512 devices in a mesh: section: 8 (over y, x_hi), patch: 64 (over z, x_lo, core).
Axes of the slice: x: 4 (x_hi: 2, x_lo: 2; x = x_hi * 2 + x_lo), y: 4, z: 16, core: 2. Of those that a mesh axis runs over, the one named last changes fastest.
Arguments:
- states: bfloat16 [8, 128, 3072], P('section', 'patch'), may hold values from -6 to 6
- w_qkv: bfloat16 [8, 3072, 4608], P('section', None, 'patch'), may hold values from -0.109375 to 0.109375
- w_out: bfloat16 [8, 1536, 3072], P('section', None, 'patch'), may hold values from -0.15625 to 0.15625
- mod_table: float32 [28, 8, 3, 3072], P(None, 'section'), may hold values from -3 to 3
- q_gain: float32 [8, 128], P('section'), may hold values from 0.5 to 2.5
- k_gain: float32 [8, 128], P('section'), may hold values from 0.5 to 2.5
- stale_kv: bfloat16 [8, 8, 128, 3072], P('section', None, 'patch'), may hold values from -6 to 6
- timestep: int32 [8], replicated, may hold values from 0 to 27
- patch_order: int32 [64], replicated, may hold values from 0 to 63, each once
Outputs:
- next_states: bfloat16 [8, 128, 3072], P('section', 'patch')
The draws below stay inside these ranges and needn't reach their ends.
Inputs may be any that keep to these rules, and one draw needn't show every extreme that they name: `patch_order`: every patch has one place, every place one patch.
All inputs are finite; a program needn't handle non-finite values.
Results may differ from the reference program's by a relative error of at most 0.015.
Values may be sent and summed in bfloat16 or wider, within the bound.
A program may use at most 64 MiB of HBM per device.

```python
import math
import jax
import jax.numpy as jnp
from jax import lax

D = 3072
HEAD_DIM = 128
TOK_DEV = 2
TICKS = 2
STEPS_TAB = 28
HD = 1536
TOKENS = 128
N_SECTION = 8
N_PATCH = 64


def with_ends(entries, own_key, low, high):
    place = [jax.random.randint(jax.random.fold_in(own_key, axis), (), 0, length) for axis, length in enumerate(entries.shape)]
    longest = entries.shape.index(max(entries.shape))
    neighbour = place[:longest] + [(place[longest] + 1) % entries.shape[longest]] + place[longest + 1:]
    return entries.at[tuple(place)].set(low).at[tuple(neighbour)].set(high)


def block_levels(own_key, shape, split, smallest, largest):
    factor_of = 1.0
    for axis_at, shards_of in split:
        draws = jax.random.uniform(jax.random.fold_in(jax.random.fold_in(own_key, 6), axis_at), (shards_of,), jnp.float32, smallest / len(split), largest / len(split))
        factor_of = factor_of * jnp.repeat(jnp.exp(draws), shape[axis_at] // shards_of).reshape((-1,) + (1,) * (len(shape) - 1 - axis_at))
    return factor_of


def scatter_about(own_key, shape, scale, limit, split=(), kind=jnp.bfloat16):
    level = block_levels(own_key, shape, split, -0.22, 0.18) if split else 1.0
    entries = jax.random.normal(own_key, shape, jnp.float32) * scale * level
    return jnp.minimum(jnp.maximum(entries, -limit), limit).astype(kind)


def setup_inputs(seed: int = 0) -> dict:
    key_of = jax.random.split(jax.random.key(seed), 10)
    states = scatter_about(key_of[0], (N_SECTION, TOKENS, D), 1.0, 6.0, ((0, 8), (1, 64)))
    w_qkv = scatter_about(key_of[1], (N_SECTION, D, 3 * HD), D ** -0.5, 0.109375, ((0, 8), (2, 64)))
    w_out = scatter_about(key_of[2], (N_SECTION, HD, D), HD ** -0.5, 0.15625, ((0, 8), (2, 64)))
    mod_table = scatter_about(key_of[3], (STEPS_TAB, N_SECTION, 3, D), 0.5, 3.0, ((1, 8),), jnp.float32)
    q_gain = jnp.clip(jnp.exp(math.log(2.5) - 1.609438 * jax.random.uniform(key_of[4], (N_SECTION, HEAD_DIM), jnp.float32) ** block_levels(key_of[4], (N_SECTION, HEAD_DIM), ((0, 8),), -0.2, 0.2)), 0.5, 2.5)
    k_gain = jnp.clip(jnp.exp(math.log(2.5) - 1.609438 * jax.random.uniform(key_of[5], (N_SECTION, HEAD_DIM), jnp.float32) ** block_levels(key_of[5], (N_SECTION, HEAD_DIM), ((0, 8),), -0.2, 0.2)), 0.5, 2.5)
    stale_kv = scatter_about(key_of[6], (N_SECTION, N_SECTION, TOKENS, 2 * HD), 1.0, 6.0, ((0, 8), (2, 64)))
    timestep = with_ends(jax.random.randint(key_of[7], (N_SECTION,), 0, STEPS_TAB), jax.random.fold_in(key_of[7], 1), 0, STEPS_TAB - 1).astype(jnp.int32)
    patch_order = jax.random.permutation(key_of[8], N_PATCH).astype(jnp.int32)
    return dict(states=states, w_qkv=w_qkv, w_out=w_out, mod_table=mod_table, q_gain=q_gain, k_gain=k_gain, stale_kv=stale_kv, timestep=timestep, patch_order=patch_order)


def modulate(state, row):
    values = state.astype(jnp.float32)
    center = values - lax.optimization_barrier(jnp.mean(values, axis=-1, keepdims=True))
    spread = lax.optimization_barrier(jnp.mean(center * center, axis=-1, keepdims=True))
    normed = center * lax.rsqrt(spread + 1e-06)
    return (normed * (1.0 + row[1]) + row[0]).astype(jnp.bfloat16)

def head_norm(values, gain):
    square = lax.optimization_barrier(jnp.mean(values * values, axis=-1, keepdims=True))
    return values * lax.rsqrt(square + 1e-06) * gain

def rotate(values, positions):
    half = values.shape[-1] // 2
    freq = jnp.exp(-jnp.log(10000.0) * jnp.arange(half, dtype=jnp.float32) / half)
    angle = positions[:, None] * freq[None, :]
    cosine = jnp.cos(angle)[:, None, :]
    sine = jnp.sin(angle)[:, None, :]
    first = values[..., :half]
    second = values[..., half:]
    return jnp.concatenate([first * cosine - second * sine, first * sine + second * cosine], axis=-1)

def block(state, w_qkv, w_out, row, q_gain, k_gain, cache, positions, patch_ids):
    count = state.shape[0]
    width = cache.shape[1] // 2
    dim = q_gain.shape[0]
    heads = width // dim
    mixed = modulate(state, row)
    qkv = jnp.dot(mixed, w_qkv, preferred_element_type=jnp.float32).astype(jnp.bfloat16)
    query = qkv[:, :width].astype(jnp.float32).reshape(count, heads, dim)
    key = qkv[:, width:2 * width].astype(jnp.float32).reshape(count, heads, dim)
    value = qkv[:, 2 * width:].astype(jnp.float32).reshape(count, heads, dim)
    query = rotate(head_norm(query, q_gain), positions).astype(jnp.bfloat16).astype(jnp.float32)
    key = rotate(head_norm(key, k_gain), positions).astype(jnp.bfloat16).astype(jnp.float32)
    stale_key = cache[:, :width].astype(jnp.float32).reshape(count, heads, dim)
    stale_value = cache[:, width:].astype(jnp.float32).reshape(count, heads, dim)
    same = patch_ids[:, None] == patch_ids[None, :]
    factor = dim ** (-0.5)
    stale_scores = jnp.einsum('qhd,khd->qhk', query, stale_key) * factor
    stale_scores = jnp.where(same[:, None, :], -1e+30, stale_scores)
    fresh_scores = jnp.einsum('qhd,khd->qhk', query, key) * factor
    fresh_scores = jnp.where(same[:, None, :], fresh_scores, -1e+30)
    top = jnp.maximum(lax.optimization_barrier(jnp.max(stale_scores, axis=-1)), lax.optimization_barrier(jnp.max(fresh_scores, axis=-1)))
    stale_weights = jnp.exp(stale_scores - top[..., None])
    fresh_weights = jnp.exp(fresh_scores - top[..., None])
    total = lax.optimization_barrier(jnp.sum(stale_weights, axis=-1)) + lax.optimization_barrier(jnp.sum(fresh_weights, axis=-1))
    summed = jnp.einsum('qhk,khd->qhd', stale_weights, stale_value) + jnp.einsum('qhk,khd->qhd', fresh_weights, value)
    attended = (summed / total[..., None]).astype(jnp.bfloat16).reshape(count, width)
    projected = jnp.dot(attended, w_out, preferred_element_type=jnp.float32)
    return (state.astype(jnp.float32) + row[2] * projected).astype(jnp.bfloat16)

def reference(states, w_qkv, w_out, mod_table, q_gain, k_gain, stale_kv, timestep, patch_order):
    sections = states.shape[0]
    token_ids = jnp.arange(TOKENS, dtype=jnp.int32)
    patch_ids = token_ids // TOK_DEV
    positions = (patch_order[patch_ids] * TOK_DEV + token_ids % TOK_DEV).astype(jnp.float32)
    for tick in range(TICKS):
        results = []
        for section in range(sections):
            image = (section - tick) % sections
            row = mod_table[timestep[image], section]
            cache = stale_kv[section, image]
            results.append(block(states[section], w_qkv[section], w_out[section], row, q_gain[section], k_gain[section], cache, positions, patch_ids))
        states = jnp.roll(jnp.stack(results), 1, axis=0)
    return states
```

```python
import functools

import jax
import jax.numpy as jnp
from jax import lax
from jax.experimental import pallas as pl
from jax.experimental.pallas import tpu as pltpu
from jax.sharding import PartitionSpec as P

MESH = pl.DeviceIdType.MESH
F32 = jnp.float32
BF16 = jnp.bfloat16
NZ = 16
NS = 8
BLK = 48
HEADS = 12
D = 3072
KC = D // 128
QROWS = 72
LAG = 4


def owner_of(head):
    part = (head % 3) * HEADS + head
    centre = (128 * part + 64) // QROWS
    return (centre // 4) * 4 + head % 4


def dot_nt(a, b):
    return lax.dot_general(a, b, (((1,), (1,)), ((), ())), preferred_element_type=F32)


def dot_nn(a, b):
    return lax.dot_general(a, b, (((1,), (0,)), ((), ())), preferred_element_type=F32)


def kernel(
    x_hbm, wq_hbm, wo_hbm, mod_hbm, st_hbm, order_ref, qg_ref, kg_ref, time_ref,
    out_ref,
    x_in, wq, wo, mod, st_in, rows_f, st_src, gran_f,
    g0, g1, wide, xr, wmod, pick, colv, table, gains,
    qsrc, qrecv, stale, stale_f, keys, vals, att, ysrc, dsrc, drecv,
    load_sem, ready, nready,
    ag_send, ag_own, ag_x, ag_core, ag_diag,
    st_send, st_recv, q_send, q_recv,
    at_send, at_own, at_x, at_core, at_diag,
    d_send, d_recv,
):
    s = lax.axis_index("section")
    p = lax.axis_index("patch")
    z = p // 4
    cls = p % 4
    xl = cls // 2
    core = p % 2
    after = (s + 1) % NS
    before = (s + NS - 1) % NS
    zbase = z * 4
    core_mate = zbase + xl * 2 + (1 - core)
    x_mate = zbase + (1 - xl) * 2 + core
    diag_mate = zbase + (1 - xl) * 2 + (1 - core)

    loads = [
        pltpu.make_async_copy(x_hbm, x_in, load_sem.at[0]),
        pltpu.make_async_copy(st_hbm.at[s], st_in.at[0], load_sem.at[1]),
        pltpu.make_async_copy(st_hbm.at[before], st_in.at[1], load_sem.at[2]),
        pltpu.make_async_copy(wq_hbm, wq, load_sem.at[3]),
        pltpu.make_async_copy(mod_hbm, mod, load_sem.at[4]),
        pltpu.make_async_copy(wo_hbm, wo, load_sem.at[5]),
    ]
    for load in loads:
        load.start()

    barrier = pltpu.get_barrier_semaphore()

    def greet(sec, dev):
        pl.semaphore_signal(barrier, inc=1, device_id=(sec, dev), device_id_type=MESH)

    def greet_line(i, _):
        greet(s, ((z + i) % NZ) * 4 + cls)
        return 0

    lax.fori_loop(1, NZ, greet_line, 0)
    for mate in (core_mate, x_mate, diag_mate):
        greet(s, mate)
    greet(after, p)
    greet(before, p)

    loads[0].wait()
    xf = x_in[...].astype(F32)
    for t in range(2):
        for k in range(KC):
            rows_f[pl.ds(t * KC + k, 1), :] = xf[t : t + 1, k * 128 : (k + 1) * 128]
    own = pl.ds(pl.multiple_of(p * BLK, 16), BLK)
    g0[own, :] = rows_f[...].astype(BF16)
    loads[1].wait()
    loads[2].wait()
    for tick in range(2):
        sf = st_in[tick].astype(F32)
        for kv in range(2):
            for head in range(HEADS):
                for t in range(2):
                    row = (head // 2) * 16 + (((head % 2) * 2 + tick) * 2 + kv) * 2 + t
                    low = (kv * HEADS + head) * 128
                    gran_f[pl.ds(row, 1), :] = sf[t : t + 1, low : low + 128]
    st_src[...] = gran_f[...].astype(BF16)

    pl.semaphore_wait(barrier, 20)

    def block(g, b):
        return g.at[pl.ds(pl.multiple_of(b * BLK, 16), BLK)]

    def push(src, dst, send, recv, sec, dev):
        pltpu.make_async_remote_copy(
            src_ref=src, dst_ref=dst, send_sem=send, recv_sem=recv,
            device_id=(sec, dev), device_id_type=MESH,
        ).start()

    def take(ref, sem):
        pltpu.make_async_copy(ref, ref, sem).wait()

    def line_z(i):
        far = (i + 1) // 2
        return (z + NZ + far * (2 * (i % 2) - 1)) % NZ

    def relay_own(g, tick, zs):
        b = zs * 4 + cls
        push(block(g, b), block(g, b), ag_send.at[tick], ag_core.at[tick], s, core_mate)
        push(block(g, b), block(g, b), ag_send.at[tick], ag_x.at[tick, zs], s, x_mate)

    def relay_x(g, tick, zs):
        b = zs * 4 + (1 - xl) * 2 + core
        take(block(g, b), ag_x.at[tick, zs])
        push(block(g, b), block(g, b), ag_send.at[tick], ag_diag.at[tick], s, core_mate)

    def relay_steps(g, tick, first, last):
        def step(i, _):
            zs = line_z(i)
            take(block(g, zs * 4 + cls), ag_own.at[tick, zs])
            relay_own(g, tick, zs)

            @pl.when(i >= LAG)
            def _():
                relay_x(g, tick, line_z(i - LAG))

            return 0

        lax.fori_loop(first, last, step, 0)

    def relay_tail(g, tick):
        def step(i, _):
            relay_x(g, tick, line_z(i))
            return 0

        lax.fori_loop(NZ - LAG, NZ, step, 0)
        some = g.at[pl.ds(0, NZ * BLK)]
        take(some, ag_core.at[tick])
        take(some, ag_diag.at[tick])

    def first_send(i, _):
        dev = line_z(NZ - i) * 4 + cls
        push(g0.at[own], g0.at[own], ag_send.at[0], ag_own.at[0, z], s, dev)
        return 0

    lax.fori_loop(1, NZ, first_send, 0)
    for mate in (core_mate, x_mate, diag_mate):
        pl.semaphore_signal(ready, inc=1, device_id=(s, mate), device_id_type=MESH)
    relay_own(g0, 0, z)
    pl.semaphore_wait(ready, 3)
    pl.semaphore_signal(nready, inc=1, device_id=(before, p), device_id_type=MESH)

    for head in range(HEADS):
        dev = owner_of(head)
        src = st_src.at[pl.ds((head // 2) * 16, 16)]
        dst = stale.at[pl.ds(pl.multiple_of(p * 16, 16), 16)]

        @pl.when(p == dev)
        def _():
            pltpu.make_async_copy(src, dst, st_recv).start()

        @pl.when(p != dev)
        def _():
            push(src, dst, st_send, st_recv, s, dev)

    my_head = jnp.int32(0)
    owned = jnp.int32(0)
    for head in range(HEADS):
        hit = jnp.where(p == owner_of(head), 1, 0)
        my_head = my_head + head * hit
        owned = owned + hit

    for load in loads[3:]:
        load.wait()
    times = [time_ref[s], time_ref[before]]
    feature = lax.broadcasted_iota(jnp.int32, (BLK, 128), 1)
    mine = p * BLK + lax.broadcasted_iota(jnp.int32, (BLK, 128), 0)
    for k in range(KC):
        lanes = pl.ds(k * 128, 128)
        pick[:, lanes] = jnp.where(feature + k * 128 == mine, 1.0, 0.0).astype(BF16)
    for tick in range(2):
        shift_sum = jnp.zeros((QROWS, 128), F32)
        row_sum = jnp.zeros((QROWS, 128), F32)
        gate_sum = jnp.zeros((BLK, 128), F32)
        base = times[tick] * 3
        for k in range(KC):
            lanes = pl.ds(k * 128, 128)
            shift = mod[base, :, lanes]
            scale = mod[base + 1, :, lanes]
            gate = mod[base + 2, :, lanes]
            w = wq[:, lanes].astype(F32)
            scaled = (w * (1.0 + scale)).astype(BF16)
            wmod[tick, :, lanes] = scaled
            shift_sum += w * shift
            row_sum += scaled.astype(F32)
            gate_sum += jnp.where(pick[:, lanes].astype(F32) > 0.5, gate, 0.0)
        for j, value in enumerate((shift_sum, row_sum)):
            total = jnp.sum(value, axis=1, keepdims=True)
            colv[tick, j, pl.ds(0, QROWS), :] = jnp.broadcast_to(total, (QROWS, 128))
        total = jnp.sum(gate_sum, axis=1, keepdims=True)
        colv[tick, 2, pl.ds(0, BLK), :] = jnp.broadcast_to(total, (BLK, 128))

    @pl.when(owned == 1)
    def _():
        r = lax.broadcasted_iota(jnp.int32, (128, 128), 0)
        c = lax.broadcasted_iota(jnp.int32, (128, 128), 1)
        for j, ref in enumerate((qg_ref, kg_ref)):
            diag = jnp.where(r == c, jnp.broadcast_to(ref[...], (128, 128)), 0.0)
            gains[j] = jnp.broadcast_to(jnp.sum(diag, axis=1, keepdims=True), (128, 128))
        pr = lax.broadcasted_iota(jnp.int32, (64, 128), 0)
        pc = lax.broadcasted_iota(jnp.int32, (64, 128), 1)
        low = jnp.where(pc < 64, pc, pc - 64)
        column = order_ref[...].astype(F32)
        place = jnp.sum(jnp.where(pr == low, column, 0.0), axis=0, keepdims=True)
        pos = place * 2.0 + jnp.where(pc[:1] < 64, 0.0, 1.0)
        freq = jnp.exp(pr.astype(F32) * (-jnp.log(F32(10000.0)) / 64.0))
        angle = pos * freq
        table[0] = jnp.cos(angle)
        table[1] = jnp.sin(angle)

    relay_steps(g0, 0, 1, NZ)
    relay_tail(g0, 0)

    def send_qkv(tick):
        for i in range(9):
            unit = p * 9 + i
            part = unit // 16
            head = part % HEADS
            dev = owner_of(head)
            kind = part // HEADS
            row = pl.multiple_of(kind * 128 + (unit % 16) * 8, 8)
            src = qsrc.at[tick, pl.ds(i * 8, 8)]
            dst = qrecv.at[tick, pl.ds(row, 8)]

            @pl.when(p == dev)
            def _():
                pltpu.make_async_copy(src, dst, q_recv.at[tick]).start()

            @pl.when(p != dev)
            def _():
                push(src, dst, q_send.at[tick], q_recv.at[tick], s, dev)

    def finish_qkv(tick, acc, mean, var):
        rstd = lax.rsqrt(var + 1e-06)
        shift = colv[tick, 0, pl.ds(0, QROWS), :]
        rows = colv[tick, 1, pl.ds(0, QROWS), :]
        qkv = rstd * (acc - rows * mean) + shift
        qsrc[tick] = qkv.astype(BF16).astype(F32)

    for b in range(24):
        part = pl.ds(b * 128, 128)
        wide[part, :] = g0[part, :].astype(F32)
    total = jnp.zeros((128, 128), F32)
    for k in range(KC):
        piece = jnp.concatenate(
            [wide[pl.ds(k, 64, stride=BLK), :], wide[pl.ds(KC + k, 64, stride=BLK), :]],
            axis=0,
        )
        total += piece
        xr[:, pl.ds(k * 128, 128)] = piece.astype(BF16)
    acc0 = dot_nt(wmod[0], xr[...])
    mean_c = jnp.sum(total, axis=1, keepdims=True) * (1.0 / D)
    total = jnp.zeros((128, 128), F32)
    for k in range(KC):
        centred = xr[:, pl.ds(k * 128, 128)].astype(F32) - mean_c
        total += centred * centred
    var_c = jnp.sum(total, axis=1, keepdims=True) * (1.0 / D)
    lane = lax.broadcasted_iota(jnp.int32, (128, 128), 1)
    stats = jnp.transpose(jnp.where(lane < 64, mean_c, var_c))
    finish_qkv(0, acc0, stats[0:1, :], stats[64:65, :])
    send_qkv(0)
    x_own = dot_nt(pick[...], xr[...])

    @pl.when(owned == 1)
    def _():
        take(stale, st_recv)
        for b in range(8):
            part = pl.ds(b * 128, 128)
            stale_f[part, :] = stale[part, :].astype(F32)
        second = my_head % 2
        for tick in range(2):
            got = []
            for kv in range(2):
                both = [
                    stale_f[pl.ds(second * 8 + (tick * 2 + kv) * 2 + t, 64, stride=16), :]
                    for t in range(2)
                ]
                got.append(jnp.concatenate(both, axis=0))
            keys[tick] = got[0].astype(BF16)
            vals[tick] = jnp.transpose(got[1]).astype(BF16)

    def attend(tick):
        take(qrecv.at[tick], q_recv.at[tick])
        factor = 128.0 ** -0.5
        cosine, sine = table[0], table[1]

        def prepared(low, j):
            u = qrecv[tick, pl.ds(low, 128), :]
            square = jnp.sum(u * u, axis=0, keepdims=True) * (1.0 / 128)
            u = u * lax.rsqrt(square + 1e-06) * gains[j]
            a, b = u[:64], u[64:]
            return jnp.concatenate(
                [a * cosine - b * sine, a * sine + b * cosine], axis=0
            ).astype(BF16)

        query = prepared(0, 0)
        key = prepared(128, 1).astype(F32)
        value = qrecv[tick, pl.ds(256, 128), :]
        scores = dot_nn(keys[tick], query) * factor
        r = lax.broadcasted_iota(jnp.int32, (128, 128), 0)
        c = lax.broadcasted_iota(jnp.int32, (128, 128), 1)
        away = jnp.abs(r - c)
        scores = jnp.where((away == 0) | (away == 64), -1e30, scores)
        wide_q = query.astype(F32)
        same = jnp.sum(wide_q * key, axis=0, keepdims=True) * factor
        other = jnp.sum(wide_q * pltpu.roll(key, 64, 1), axis=0, keepdims=True) * factor
        top = jnp.maximum(jnp.max(scores, axis=0, keepdims=True), jnp.maximum(same, other))
        weights = jnp.exp(scores - top)
        same = jnp.exp(same - top)
        other = jnp.exp(other - top)
        mass = jnp.sum(weights, axis=0, keepdims=True) + same + other
        summed = dot_nn(vals[tick], weights.astype(BF16))
        summed = summed + same * value + other * pltpu.roll(value, 64, 1)
        rows = pl.ds(pl.multiple_of(my_head * 128, 128), 128)
        att[tick, rows, :] = (summed / mass).astype(BF16)

        def send(i, _):
            dev = line_z(NZ - i) * 4 + cls
            piece = att.at[tick, rows]
            push(piece, piece, at_send.at[tick], at_own.at[tick, my_head // 4], s, dev)
            return 0

        lax.fori_loop(1, NZ, send, 0)

    def head_rows(tick, head):
        return att.at[tick, pl.ds(pl.multiple_of(head * 128, 128), 128)]

    def gather_attended(tick):
        for j in range(3):
            head = j * 4 + cls
            piece = head_rows(tick, head)

            @pl.when(owner_of(head) != p)
            def _():
                take(piece, at_own.at[tick, j])

            push(piece, piece, at_send.at[tick], at_core.at[tick], s, core_mate)
            push(piece, piece, at_send.at[tick], at_x.at[tick, j], s, x_mate)
        for j in range(3):
            head = j * 4 + (1 - xl) * 2 + core
            piece = head_rows(tick, head)
            take(piece, at_x.at[tick, j])
            push(piece, piece, at_send.at[tick], at_diag.at[tick], s, core_mate)
        some = att.at[tick, pl.ds(0, 3 * 128)]
        take(some, at_core.at[tick])
        take(some, at_diag.at[tick])

    def project(tick, residual):
        out = dot_nn(wo[...], att[tick])
        gate = colv[tick, 2, pl.ds(0, BLK), :]
        return (residual + gate * out).astype(BF16)

    @pl.when(owned == 1)
    def _():
        attend(0)

    gather_attended(0)
    ysrc[...] = project(0, x_own)

    pl.semaphore_wait(nready, 1)

    def second_send(i, _):
        dev = line_z(NZ - i) * 4 + cls
        push(ysrc, g1.at[own], ag_send.at[1], ag_own.at[1, z], after, dev)
        return 0

    lax.fori_loop(1, NZ + 1, second_send, 0)

    relay_steps(g1, 1, 0, NZ)
    relay_tail(g1, 1)
    acc1 = dot_nn(wmod[1], g1[...])
    total = jnp.zeros((128, 128), F32)
    for k in range(KC):
        total += g1[pl.ds(k * 128, 128), :].astype(F32)
    mean = jnp.sum(total, axis=0, keepdims=True) * (1.0 / D)
    total = jnp.zeros((128, 128), F32)
    for k in range(KC):
        centred = g1[pl.ds(k * 128, 128), :].astype(F32) - mean
        total += centred * centred
    var = jnp.sum(total, axis=0, keepdims=True) * (1.0 / D)
    finish_qkv(1, acc1, mean, var)
    send_qkv(1)

    @pl.when(owned == 1)
    def _():
        attend(1)

    gather_attended(1)
    last = project(1, g1[own, :].astype(F32)).astype(F32)
    stacked = jnp.concatenate(
        [last, pltpu.roll(last, 64, 1), jnp.zeros((32, 128), F32)], axis=0
    )
    turned = jnp.transpose(stacked)
    for i in range(64):
        dsrc[i] = turned[i : i + 1, :]

    def last_send(i, _):
        dev = (p + i) % 64
        push(dsrc.at[dev], drecv.at[p], d_send, d_recv, after, dev)
        return 0

    lax.fori_loop(0, 64, last_send, 0)
    take(drecv, d_recv)
    out_ref[...] = drecv[...]

    take(g0.at[pl.ds(0, 63 * BLK)], ag_send.at[0])
    take(g1, ag_send.at[1])
    take(dsrc, d_send)
    is_owner = owned == 1
    mine_units = jnp.int32(0)
    for i in range(9):
        mine_units = mine_units + jnp.where(
            owner_of(((p * 9 + i) // 16) % HEADS) == p, 1, 0
        )
    for tick in range(2):
        def drain(i, _):
            take(qsrc.at[tick, pl.ds(0, 8)], q_send.at[tick])
            return 0

        lax.fori_loop(0, 9 - mine_units, drain, 0)
        take(att.at[tick, pl.ds(0, 9 * 128)], at_send.at[tick])

        @pl.when(is_owner)
        def _():
            def drain_piece(i, _):
                take(att.at[tick, pl.ds(0, 128)], at_send.at[tick])
                return 0

            lax.fori_loop(1, NZ, drain_piece, 0)

    def drain_stale(i, _):
        take(st_src.at[pl.ds(0, 16)], st_send)
        return 0

    lax.fori_loop(0, HEADS - owned, drain_stale, 0)


def per_device(states, w_qkv, w_out, mod_table, q_gain, k_gain, stale_kv, timestep, patch_order):
    hbm = pl.BlockSpec(memory_space=pl.ANY)
    vmem = pl.BlockSpec(memory_space=pltpu.VMEM)
    dma = pltpu.SemaphoreType.DMA
    regular = pltpu.SemaphoreType.REGULAR
    got = pl.pallas_call(
        kernel,
        out_shape=jax.ShapeDtypeStruct((64, 1, 128), F32),
        in_specs=[hbm] * 5 + [vmem] * 3 + [pl.BlockSpec(memory_space=pltpu.SMEM)],
        out_specs=vmem,
        scratch_shapes=[
            pltpu.VMEM((2, D), BF16),
            pltpu.VMEM((QROWS, D), BF16),
            pltpu.VMEM((BLK, D // 2), BF16),
            pltpu.VMEM((84, 1, D), F32),
            pltpu.VMEM((2, 2, D), BF16),
            pltpu.VMEM((BLK, 128), F32),
            pltpu.VMEM((96, 128), BF16),
            pltpu.VMEM((96, 128), F32),
            pltpu.VMEM((D, 128), BF16),
            pltpu.VMEM((D, 128), BF16),
            pltpu.VMEM((D, 128), F32),
            pltpu.VMEM((128, D), BF16),
            pltpu.VMEM((2, QROWS, D), BF16),
            pltpu.VMEM((BLK, D), BF16),
            pltpu.VMEM((2, 3, QROWS, 128), F32),
            pltpu.VMEM((2, 64, 128), F32),
            pltpu.VMEM((2, 128, 128), F32),
            pltpu.VMEM((2, QROWS, 128), F32),
            pltpu.VMEM((2, 384, 128), F32),
            pltpu.VMEM((1024, 128), BF16),
            pltpu.VMEM((1024, 128), F32),
            pltpu.VMEM((2, 128, 128), BF16),
            pltpu.VMEM((2, 128, 128), BF16),
            pltpu.VMEM((2, D // 2, 128), BF16),
            pltpu.VMEM((BLK, 128), BF16),
            pltpu.VMEM((64, 1, 128), F32),
            pltpu.VMEM((64, 1, 128), F32),
            dma((6,)),
            regular,
            regular,
            dma((2,)),
            dma((2, NZ)),
            dma((2, NZ)),
            dma((2,)),
            dma((2,)),
            dma,
            dma,
            dma((2,)),
            dma((2,)),
            dma((2,)),
            dma((2, 3)),
            dma((2, 3)),
            dma((2,)),
            dma((2,)),
            dma,
            dma,
        ],
        compiler_params=pltpu.CompilerParams(
            collective_id=0, has_side_effects=True, vmem_limit_bytes=40 * 2**20
        ),
        name="block_cycle",
    )(
        states[0],
        w_qkv[0].T,
        w_out[0].T,
        jnp.transpose(mod_table, (0, 2, 1, 3)).reshape(84, 1, D),
        stale_kv[0],
        patch_order.reshape(64, 1),
        q_gain,
        k_gain,
        timestep,
    )
    pairs = got[:, 0, : 2 * BLK].reshape(64, 2, BLK)
    return jnp.transpose(pairs, (1, 0, 2)).reshape(1, 2, D).astype(BF16)


def solution(mesh):
    in_specs = (
        P("section", "patch", None),
        P("section", None, "patch"),
        P("section", None, "patch"),
        P(None, "section", None, None),
        P("section", None),
        P("section", None),
        P("section", None, "patch", None),
        P(),
        P(),
    )
    out_specs = P("section", "patch", None)
    return jax.shard_map(
        per_device, mesh=mesh, in_specs=in_specs, out_specs=out_specs, check_vma=False
    )
```

```python
import jax
import jax.numpy as jnp
from jax import lax
from jax.experimental import pallas as pl
from jax.experimental.pallas import tpu as pltpu
from jax.sharding import PartitionSpec as P

MESH = pl.DeviceIdType.MESH
F32 = jnp.float32
BF16 = jnp.bfloat16
NZ = 16
NS = 8
BLK = 48
HEADS = 12
PAIRS = 6
D = 3072
KC = D // 128
LINE = 32
QROWS = 72
REACH = 4
CHUNK = 768


def owner_of(pair, line):
    part = ((pair + line) % 3) * PAIRS + pair
    centre = (32 * part + 16) // 9
    return (centre // 4) * 4 + 2 * line + pair % 2


def dot_nt(a, b):
    return lax.dot_general(a, b, (((1,), (1,)), ((), ())), preferred_element_type=F32)


def dot_nn(a, b):
    return lax.dot_general(a, b, (((1,), (0,)), ((), ())), preferred_element_type=F32)


def kernel(
    x_hbm, wq_hbm, wo_hbm, mod_hbm, st_hbm, order_ref, qg_ref, kg_ref, time_ref,
    out_ref,
    x_in, wq, wo, mod, st_in, rows_f, st_src, gran_f,
    g0, g1, wide, xr, wmod, wodd, weven, perm, wlow, whigh, pick, colv, gatev, table, gains,
    qsrc, qrecv, stale, stale_f, keys, vals, att, ysrc, dsrc, drecv,
    load_sem, ready, nready, w_send, w_recv,
    ag_send, ag_own, ag_core,
    st_send, st_recv, q_send, q_recv,
    at_send, at_own, at_core,
    d_send, d_recv,
):
    s = lax.axis_index("section")
    p = lax.axis_index("patch")
    z = p // 4
    xl = (p // 2) % 2
    core = p % 2
    me = z * 2 + core
    after = (s + 1) % NS
    before = (s + NS - 1) % NS
    core_mate = z * 4 + xl * 2 + (1 - core)
    x_mate = z * 4 + (1 - xl) * 2 + core
    diag_mate = z * 4 + (1 - xl) * 2 + (1 - core)

    def on_line(zs, c):
        return zs * 4 + xl * 2 + c

    loads = [
        pltpu.make_async_copy(x_hbm, x_in, load_sem.at[0]),
        pltpu.make_async_copy(st_hbm.at[s], st_in.at[0], load_sem.at[1]),
        pltpu.make_async_copy(st_hbm.at[before], st_in.at[1], load_sem.at[2]),
        pltpu.make_async_copy(wq_hbm, wq.at[xl], load_sem.at[3]),
        pltpu.make_async_copy(wo_hbm, wo.at[xl], load_sem.at[4]),
        pltpu.make_async_copy(mod_hbm, mod, load_sem.at[5]),
    ]
    for load in loads:
        load.start()

    barrier = pltpu.get_barrier_semaphore()

    def greet(sec, dev):
        pl.semaphore_signal(barrier, inc=1, device_id=(sec, dev), device_id_type=MESH)

    def greet_line(i, _):
        greet(s, on_line((z + i) % NZ, core))
        return 0

    lax.fori_loop(1, NZ, greet_line, 0)
    for mate in (core_mate, x_mate, diag_mate):
        greet(s, mate)
    greet(after, p)
    greet(before, p)

    loads[0].wait()
    xf = x_in[...].astype(F32)
    for t in range(2):
        for k in range(KC):
            rows_f[pl.ds(t * KC + k, 1), :] = xf[t : t + 1, k * 128 : (k + 1) * 128]
    own = pl.ds(pl.multiple_of(me * BLK, 16), BLK)
    g0[own, :] = rows_f[...].astype(BF16)
    loads[1].wait()
    loads[2].wait()
    for tick in range(2):
        sf = st_in[tick].astype(F32)
        for kv in range(2):
            for head in range(HEADS):
                for t in range(2):
                    row = (head // 2) * 16 + (((head % 2) * 2 + tick) * 2 + kv) * 2 + t
                    low = (kv * HEADS + head) * 128
                    gran_f[pl.ds(row, 1), :] = sf[t : t + 1, low : low + 128]
    st_src[...] = gran_f[...].astype(BF16)
    for load in loads[3:]:
        load.wait()

    def block(g, b):
        return g.at[pl.ds(pl.multiple_of(b * BLK, 16), BLK)]

    def push(src, dst, send, recv, sec, dev):
        pltpu.make_async_remote_copy(
            src_ref=src, dst_ref=dst, send_sem=send, recv_sem=recv,
            device_id=(sec, dev), device_id_type=MESH,
        ).start()

    def take(ref, sem):
        pltpu.make_async_copy(ref, ref, sem).wait()

    my_pair = jnp.int32(0)
    owned = jnp.int32(0)
    for pair in range(PAIRS):
        hit = jnp.where(p == owner_of(pair, xl), 1, 0)
        my_pair = my_pair + pair * hit
        owned = owned + hit

    def finish(stage):
        if stage == 2:
            @pl.when(owned == 1)
            def _():
                take(stale, st_recv)
        if 2 <= stage < 5:
            pl.semaphore_wait(nready, 1)
        if stage >= 2:
            take(g0.at[pl.ds(0, 31 * BLK)], ag_send.at[0])
            take(wq.at[xl], w_send.at[0])
            take(wo.at[xl], w_send.at[1])

            def drain_stale(i, _):
                take(st_src.at[pl.ds(0, 16)], st_send)
                return 0

            lax.fori_loop(0, 2 * PAIRS - owned, drain_stale, 0)
        if 2 <= stage < 4:
            take(wo.at[1 - xl], w_recv.at[1])
        if stage >= 5:
            take(g1, ag_send.at[1])
        if stage >= 8:
            take(dsrc, d_send)
        mine_units = jnp.int32(0)
        for j in range(2):
            for i in range(9):
                unit = (z * 4 + 2 * j + core) * 9 + i
                pair = ((unit // 16) % HEADS) // 2
                mine_units = mine_units + jnp.where(owner_of(pair, xl) == p, 1, 0)
        for tick in range(2):
            def drain(i, _):
                take(qsrc.at[tick, 0, pl.ds(0, 8)], q_send.at[tick])
                return 0

            if stage >= 3 + 3 * tick:
                lax.fori_loop(0, 18 - mine_units, drain, 0)
            if stage >= 4 + 3 * tick:
                def drain_piece(i, _):
                    take(att.at[tick, pl.ds(0, 128)], at_send.at[tick])
                    return 0

                lax.fori_loop(0, 3 + (NZ - 1) * owned, drain_piece, 0)

    def relay_core(g, tick, zs):
        b = zs * 2 + core
        push(block(g, b), block(g, b), ag_send.at[tick], ag_core.at[tick], s, core_mate)

    def arrive(g, tick, i):
        far = (i + 1) // 2
        zs = (z + NZ - far * (2 * (i % 2) - 1)) % NZ
        take(block(g, zs * 2 + core), ag_own.at[tick, zs])
        return zs

    def near_step(g, tick):
        def step(i, _):
            relay_core(g, tick, arrive(g, tick, i))
            return 0

        return step

    def relay(g, tick, first):
        lax.fori_loop(first, 2 * REACH - 1, near_step(g, tick), 0)
        for i in (2 * REACH - 1, 2 * REACH):
            zs = arrive(g, tick, i)
            sign = 2 * (i % 2) - 1
            piece = block(g, zs * 2 + core)
            for far in range(REACH - 1 + i % 2, 0, -1):
                dev = on_line((z + NZ + sign * far) % NZ, core)
                push(piece, piece, ag_send.at[tick], ag_own.at[tick, zs], s, dev)
            relay_core(g, tick, zs)
        lax.fori_loop(2 * REACH + 1, NZ, near_step(g, tick), 0)
        take(g.at[pl.ds(0, NZ * BLK)], ag_core.at[tick])

    def spread(src, dst, tick, sec, first):
        def send(far, sign):
            dev = on_line((z + NZ + sign * far) % NZ, core)
            push(src, dst, ag_send.at[tick], ag_own.at[tick, z], sec, dev)

        send(REACH, 1)
        send(REACH, -1)
        if first == 0:
            send(0, 1)
        for far in range(1, REACH):
            send(far, 1)
            send(far, -1)

    pl.semaphore_wait(barrier, 20)

    spread(g0.at[own], g0.at[own], 0, s, 1)
    push(wq.at[xl], wq.at[xl], w_send.at[0], w_recv.at[0], s, x_mate)
    push(wo.at[xl], wo.at[xl], w_send.at[1], w_recv.at[1], s, x_mate)
    for mate in (core_mate, x_mate, diag_mate):
        pl.semaphore_signal(ready, inc=1, device_id=(s, mate), device_id_type=MESH)
    relay_core(g0, 0, z)

    times = [time_ref[s], time_ref[before]]
    lane = lax.broadcasted_iota(jnp.int32, (128, 128), 1)
    first_half = lane < 64

    def fold(tick, j):
        shift_sum = jnp.zeros((QROWS, 128), F32)
        row_sum = jnp.zeros((QROWS, 128), F32)
        base = times[tick] * 3
        for k in range(KC):
            lanes = pl.ds(k * 128, 128)
            shift = mod[base, :, lanes]
            scale = mod[base + 1, :, lanes]
            w = wq[j, :, lanes].astype(F32)
            scaled = (w * (1.0 + scale)).astype(BF16)
            wmod[tick, j, :, lanes] = scaled
            shift_sum += w * shift
            row_sum += scaled.astype(F32)
        for n, value in enumerate((shift_sum, row_sum)):
            total = jnp.sum(value, axis=1, keepdims=True)
            colv[tick, n, j] = jnp.broadcast_to(total, (QROWS, 128))

    fold(0, xl)

    pl.semaphore_wait(ready, 3)
    pl.semaphore_signal(nready, inc=1, device_id=(before, p), device_id_type=MESH)
    for pair in range(PAIRS):
        for line in range(2):
            dev = owner_of(pair, line)
            src = st_src.at[pl.ds(pair * 16, 16)]
            dst = stale.at[pl.ds(pl.multiple_of(p * 16, 16), 16)]

            @pl.when(p == dev)
            def _():
                pltpu.make_async_copy(src, dst, st_recv).start()

            @pl.when(p != dev)
            def _():
                push(src, dst, st_send, st_recv, s, dev)

    feature = lax.broadcasted_iota(jnp.int32, (BLK, 128), 1)
    row = lax.broadcasted_iota(jnp.int32, (BLK, 128), 0)
    gate_sums = []
    for j in range(2):
        mine = (z * 4 + 2 * j + core) * BLK + row
        sums = [jnp.zeros((BLK, 128), F32), jnp.zeros((BLK, 128), F32)]
        for k in range(KC):
            lanes = pl.ds(k * 128, 128)
            here = feature + k * 128 == mine
            pick[j, :, lanes] = jnp.where(here, 1.0, 0.0).astype(BF16)
            for tick in range(2):
                sums[tick] += jnp.where(here, mod[times[tick] * 3 + 2, :, lanes], 0.0)
        gate_sums.append([jnp.sum(v, axis=1, keepdims=True) for v in sums])
    for tick in range(2):
        gatev[tick] = jnp.where(first_half[:BLK], gate_sums[0][tick], gate_sums[1][tick])

    @pl.when(owned == 1)
    def _():
        r = lax.broadcasted_iota(jnp.int32, (128, 128), 0)
        for j, ref in enumerate((qg_ref, kg_ref)):
            diag = jnp.where(r == lane, jnp.broadcast_to(ref[...], (128, 128)), 0.0)
            gains[j] = jnp.broadcast_to(jnp.sum(diag, axis=1, keepdims=True), (128, 128))
        pr = r[:64]
        pc = lane[:64]
        places = jnp.broadcast_to(order_ref[...].astype(F32), (64, 64))
        column = jnp.sum(
            jnp.where(pr[:, :64] == pc[:, :64], places, 0.0), axis=1, keepdims=True
        )
        token = pc % 64
        patch = ((token % LINE) // 2) * 4 + 2 * xl + token % 2
        place = jnp.sum(jnp.where(pr == patch, column, 0.0), axis=0, keepdims=True)
        pos = place * 2.0 + jnp.where(token[:1] < LINE, 0.0, 1.0)
        freq = jnp.exp(pr.astype(F32) * (-jnp.log(F32(10000.0)) / 64.0))
        angle = pos * freq
        table[0] = jnp.cos(angle)
        table[1] = jnp.sin(angle)

    relay(g0, 0, 1)
    take(wq.at[1 - xl], w_recv.at[0])
    fold(0, 1 - xl)

    def send_qkv(tick):
        for j in range(2):
            for i in range(9):
                unit = (z * 4 + 2 * j + core) * 9 + i
                part = unit // 16
                head = part % HEADS
                dev = owner_of(head // 2, xl)
                kind = part // HEADS
                low = pl.multiple_of(kind * 128 + (unit % 16) * 8, 8)
                src = qsrc.at[tick, j, pl.ds(i * 8, 8)]
                dst = qrecv.at[tick, head % 2, pl.ds(low, 8)]

                @pl.when(p == dev)
                def _():
                    pltpu.make_async_copy(src, dst, q_recv.at[tick]).start()

                @pl.when(p != dev)
                def _():
                    push(src, dst, q_send.at[tick], q_recv.at[tick], s, dev)

    def finish_qkv(tick, accs, mean, var):
        rstd = lax.rsqrt(var + 1e-06)
        for j in range(2):
            qkv = rstd * (accs[j] - colv[tick, 1, j] * mean) + colv[tick, 0, j]
            qsrc[tick, j] = qkv.astype(BF16).astype(F32)

    for b in range(12):
        part = pl.ds(b * 128, 128)
        wide[part, :] = g0[part, :].astype(F32)
    total = jnp.zeros((64, 128), F32)
    for k in range(KC):
        lanes = pl.ds(k * 128, 128)
        piece = jnp.concatenate(
            [wide[pl.ds(t * KC + k, LINE, stride=BLK), :] for t in range(2)], axis=0
        )
        total += piece
        narrow = piece.astype(BF16)
        xr[pl.ds(0, 64), lanes] = narrow
        xr[pl.ds(64, 64), lanes] = narrow
    accs = [dot_nt(wmod[0, j], xr[...]) for j in range(2)]
    mean_c = jnp.sum(total, axis=1, keepdims=True) * (1.0 / D)
    total = jnp.zeros((64, 128), F32)
    for k in range(KC):
        centred = xr[pl.ds(0, 64), pl.ds(k * 128, 128)].astype(F32) - mean_c
        total += centred * centred
    var_c = jnp.sum(total, axis=1, keepdims=True) * (1.0 / D)
    stats = jnp.where(first_half[:64], mean_c, var_c)
    stats = jnp.transpose(jnp.concatenate([stats, stats], axis=0))
    finish_qkv(0, accs, stats[0:1, :], stats[64:65, :])
    send_qkv(0)

    @pl.when(owned == 1)
    def _():
        take(stale, st_recv)
        for b in range(8):
            part = pl.ds(b * 128, 128)
            stale_f[part, :] = stale[part, :].astype(F32)
        for tick in range(2):
            for second in range(2):
                got = []
                for kv in range(2):
                    both = [
                        stale_f[
                            pl.ds(((second * 2 + tick) * 2 + kv) * 2 + t, 64, stride=16), :
                        ]
                        for t in range(2)
                    ]
                    got.append(jnp.concatenate(both, axis=0))
                keys[tick, second] = got[0].astype(BF16)
                vals[tick, second] = jnp.transpose(got[1]).astype(BF16)

    def attend(tick):
        take(qrecv.at[tick], q_recv.at[tick])
        factor = 128.0 ** -0.5
        cosine, sine = table[0], table[1]

        def received(low):
            part = pl.ds(low, 128)
            return jnp.where(first_half, qrecv[tick, 0, part, :], qrecv[tick, 1, part, :])

        def prepared(low, j):
            u = received(low)
            square = jnp.sum(u * u, axis=0, keepdims=True) * (1.0 / 128)
            u = u * lax.rsqrt(square + 1e-06) * gains[j]
            a, b = u[:64], u[64:]
            return jnp.concatenate(
                [a * cosine - b * sine, a * sine + b * cosine], axis=0
            ).astype(BF16)

        def partner(u):
            up = pltpu.roll(u, 128 - LINE, 1)
            down = pltpu.roll(u, LINE, 1)
            return jnp.where(lane % 64 < LINE, up, down)

        query = prepared(0, 0)
        key = prepared(128, 1).astype(F32)
        value = received(256)
        scores = jnp.where(
            first_half, dot_nn(keys[tick, 0], query), dot_nn(keys[tick, 1], query)
        ) * factor
        r = lax.broadcasted_iota(jnp.int32, (128, 128), 0)
        patch = ((lane % LINE) // 2) * 4 + 2 * xl + lane % 2
        scores = jnp.where(r % 64 == patch, -1e30, scores)
        wide_q = query.astype(F32)
        same = jnp.sum(wide_q * key, axis=0, keepdims=True) * factor
        other = jnp.sum(wide_q * partner(key), axis=0, keepdims=True) * factor
        top = jnp.maximum(jnp.max(scores, axis=0, keepdims=True), jnp.maximum(same, other))
        weights = jnp.exp(scores - top)
        same = jnp.exp(same - top)
        other = jnp.exp(other - top)
        mass = jnp.sum(weights, axis=0, keepdims=True) + same + other
        weights = weights.astype(BF16)
        summed = jnp.where(
            first_half, dot_nn(vals[tick, 0], weights), dot_nn(vals[tick, 1], weights)
        )
        summed = summed + same * value + other * partner(value)
        att[tick, pair_rows(my_pair), :] = (summed / mass).astype(BF16)

    def pair_rows(pair):
        return pl.ds(pl.multiple_of(pair * 128, 128), 128)

    def send_attended(tick):
        piece = att.at[tick, pair_rows(my_pair)]

        def send(i, _):
            far = (NZ - i + 1) // 2
            dev = on_line((z + NZ + far * (2 * (i % 2) - 1)) % NZ, core)
            push(piece, piece, at_send.at[tick], at_own.at[tick, my_pair // 2], s, dev)
            return 0

        lax.fori_loop(1, NZ, send, 0)

    def gather_attended(tick):
        for j in range(3):
            pair = j * 2 + core
            piece = att.at[tick, pair_rows(pair)]

            @pl.when(owner_of(pair, xl) != p)
            def _():
                take(piece, at_own.at[tick, j])

            push(piece, piece, at_send.at[tick], at_core.at[tick], s, core_mate)
        take(att.at[tick, pl.ds(0, 3 * 128)], at_core.at[tick])

    def project(tick, residual):
        out = jnp.where(
            first_half[: 2 * BLK], dot_nn(weven[...], att[tick]), dot_nn(wodd[...], att[tick])
        )
        out = out + pltpu.roll(out, 64, 1)
        out = jnp.where(first_half[:BLK], out[:BLK], out[BLK:])
        return (residual + gatev[tick] * out).astype(BF16)

    @pl.when(owned == 1)
    def _():
        attend(0)

    @pl.when(owned == 1)
    def _():
        send_attended(0)

    picked = [dot_nt(pick[j], xr[...]) for j in range(2)]
    residual = jnp.where(first_half[:BLK], picked[0], picked[1])
    take(wo.at[1 - xl], w_recv.at[1])
    for j in range(2):
        for pair in range(PAIRS):
            at = pl.ds(j * BLK, BLK), pl.ds(pair * 128, 128)
            weven[at] = wo[j, :, pl.ds(pair * 256, 128)]
            wodd[at] = wo[j, :, pl.ds(pair * 256 + 128, 128)]
    pf = lax.broadcasted_iota(jnp.int32, (CHUNK, 128), 0)
    po = lax.broadcasted_iota(jnp.int32, (CHUNK, 128), 1)
    for k in range(CHUNK // 128):
        to = po + (k % 3) * 128
        group = jnp.where(to >= 96, 1, 0) + jnp.where(to >= 192, 1, 0) + jnp.where(to >= 288, 1, 0)
        source = to + 96 * group + 96 * (k // 3)
        perm[:, pl.ds(k * 128, 128)] = jnp.where(pf == source, 1.0, 0.0).astype(BF16)
    half = CHUNK // 2
    for j in range(2):
        fold(1, j)
        for k in range(D // CHUNK):
            moved = dot_nn(wmod[1, j, :, pl.ds(k * CHUNK, CHUNK)], perm[...]).astype(BF16)
            wlow[j, :, pl.ds(k * half, half)] = moved[:, :half]
            whigh[j, :, pl.ds(k * half, half)] = moved[:, half:]

    gather_attended(0)
    ysrc[...] = project(0, residual)

    pl.semaphore_wait(nready, 1)
    spread(ysrc, g1.at[own], 1, after, 0)

    relay(g1, 1, 0)
    accs = []
    for j in range(2):
        acc = jnp.where(
            first_half[:QROWS], dot_nn(wlow[j], g1[...]), dot_nn(whigh[j], g1[...])
        )
        accs.append(acc + pltpu.roll(acc, 64, 1))
    total = jnp.zeros((128, 128), F32)
    for k in range(12):
        total += g1[pl.ds(k * 128, 128), :].astype(F32)
    total = jnp.sum(total, axis=0, keepdims=True)
    mean = (total + pltpu.roll(total, 64, 1)) * (1.0 / D)
    total = jnp.zeros((128, 128), F32)
    for k in range(12):
        centred = g1[pl.ds(k * 128, 128), :].astype(F32) - mean
        total += centred * centred
    total = jnp.sum(total, axis=0, keepdims=True)
    var = (total + pltpu.roll(total, 64, 1)) * (1.0 / D)
    finish_qkv(1, accs, mean, var)
    send_qkv(1)

    @pl.when(owned == 1)
    def _():
        attend(1)

    @pl.when(owned == 1)
    def _():
        send_attended(1)

    gather_attended(1)
    last = project(1, g1[own, :].astype(F32)).astype(F32)
    blank = jnp.zeros((16, 128), F32)
    turned = jnp.transpose(
        jnp.concatenate([last, blank, pltpu.roll(last, 64, 1), blank], axis=0)
    )
    for i in range(LINE):
        for t in range(2):
            dsrc[i, pl.ds(t, 1), :] = turned[t * LINE + i : t * LINE + i + 1, :]

    def last_send(i, _):
        to = (me + i) % LINE
        push(dsrc.at[to], drecv.at[me], d_send, d_recv, after, on_line(to // 2, to % 2))
        return 0

    lax.fori_loop(0, LINE, last_send, 0)
    take(drecv, d_recv)
    out_ref[...] = drecv[...]
    finish(8)


def per_device(states, w_qkv, w_out, mod_table, q_gain, k_gain, stale_kv, timestep, patch_order):
    hbm = pl.BlockSpec(memory_space=pl.ANY)
    vmem = pl.BlockSpec(memory_space=pltpu.VMEM)
    dma = pltpu.SemaphoreType.DMA
    regular = pltpu.SemaphoreType.REGULAR
    got = pl.pallas_call(
        kernel,
        out_shape=jax.ShapeDtypeStruct((LINE, 2, 128), F32),
        in_specs=[hbm] * 5 + [vmem] * 3 + [pl.BlockSpec(memory_space=pltpu.SMEM)],
        out_specs=vmem,
        scratch_shapes=[
            pltpu.VMEM((2, D), BF16),
            pltpu.VMEM((2, QROWS, D), BF16),
            pltpu.VMEM((2, BLK, D // 2), BF16),
            pltpu.VMEM((84, 1, D), F32),
            pltpu.VMEM((2, 2, D), BF16),
            pltpu.VMEM((BLK, 128), F32),
            pltpu.VMEM((96, 128), BF16),
            pltpu.VMEM((96, 128), F32),
            pltpu.VMEM((LINE * BLK, 128), BF16),
            pltpu.VMEM((LINE * BLK, 128), BF16),
            pltpu.VMEM((LINE * BLK, 128), F32),
            pltpu.VMEM((128, D), BF16),
            pltpu.VMEM((2, 2, QROWS, D), BF16),
            pltpu.VMEM((2 * BLK, D // 4), BF16),
            pltpu.VMEM((2 * BLK, D // 4), BF16),
            pltpu.VMEM((CHUNK, CHUNK), BF16),
            pltpu.VMEM((2, QROWS, D // 2), BF16),
            pltpu.VMEM((2, QROWS, D // 2), BF16),
            pltpu.VMEM((2, BLK, D), BF16),
            pltpu.VMEM((2, 2, 2, QROWS, 128), F32),
            pltpu.VMEM((2, BLK, 128), F32),
            pltpu.VMEM((2, 64, 128), F32),
            pltpu.VMEM((2, 128, 128), F32),
            pltpu.VMEM((2, 2, QROWS, 128), F32),
            pltpu.VMEM((2, 2, 384, 128), F32),
            pltpu.VMEM((1024, 128), BF16),
            pltpu.VMEM((1024, 128), F32),
            pltpu.VMEM((2, 2, 128, 128), BF16),
            pltpu.VMEM((2, 2, 128, 128), BF16),
            pltpu.VMEM((2, PAIRS * 128, 128), BF16),
            pltpu.VMEM((BLK, 128), BF16),
            pltpu.VMEM((LINE, 2, 128), F32),
            pltpu.VMEM((LINE, 2, 128), F32),
            dma((6,)),
            regular,
            regular,
            dma((2,)),
            dma((2,)),
            dma((2,)),
            dma((2, NZ)),
            dma((2,)),
            dma,
            dma,
            dma((2,)),
            dma((2,)),
            dma((2,)),
            dma((2, 3)),
            dma((2,)),
            dma,
            dma,
        ],
        compiler_params=pltpu.CompilerParams(
            collective_id=0, has_side_effects=True, vmem_limit_bytes=56 * 2**20
        ),
        name="block_cycle",
    )(
        states[0],
        w_qkv[0].T,
        w_out[0].T,
        jnp.transpose(mod_table, (0, 2, 1, 3)).reshape(84, 1, D),
        stale_kv[0],
        patch_order.reshape(1, 64),
        q_gain,
        k_gain,
        timestep,
    )
    split = got.reshape(NZ, 2, 2, 2, 64)[..., :BLK]
    return jnp.transpose(split, (2, 0, 3, 1, 4)).reshape(1, 2, D).astype(BF16)


def solution(mesh):
    in_specs = (
        P("section", "patch", None),
        P("section", None, "patch"),
        P("section", None, "patch"),
        P(None, "section", None, None),
        P("section", None),
        P("section", None),
        P("section", None, "patch", None),
        P(),
        P(),
    )
    out_specs = P("section", "patch", None)
    return jax.shard_map(
        per_device, mesh=mesh, in_specs=in_specs, out_specs=out_specs, check_vma=False
    )
```

```python
import jax
import jax.numpy as jnp
from jax import lax
from jax.experimental import pallas as pl
from jax.experimental.pallas import tpu as pltpu
from jax.sharding import PartitionSpec as P

MESH = pl.DeviceIdType.MESH
F32 = jnp.float32
BF16 = jnp.bfloat16
NZ = 16
NS = 8
BLK = 48
HEADS = 12
PAIRS = 6
D = 3072
KC = D // 128
LINE = 32
QROWS = 72
REACH = 4
CHUNK = 768


def owner_of(pair, line):
    part = ((pair + line) % 3) * PAIRS + pair
    centre = (32 * part + 16) // 9
    return (centre // 4) * 4 + 2 * line + pair % 2


def dot_nt(a, b):
    return lax.dot_general(a, b, (((1,), (1,)), ((), ())), preferred_element_type=F32)


def dot_nn(a, b):
    return lax.dot_general(a, b, (((1,), (0,)), ((), ())), preferred_element_type=F32)


def kernel(
    x_hbm, wq_hbm, wo_hbm, mod_hbm, st_hbm, order_ref, qg_ref, kg_ref, time_ref,
    out_ref,
    x_in, wq, wo, mod, st_in, rows_f, st_src, gran_f,
    g0, g1, wide, xr, wmod, wodd, weven, perm, wlow, whigh, pick, colv, gatev, table, gains,
    qsrc, qrecv, stale, stale_f, keys, vals, att, ysrc, dsrc, drecv,
    load_sem, nready, w_send, w_recv,
    ag_send, ag_own, ag_core,
    st_send, st_recv, q_send, q_recv,
    at_send, at_own, at_core,
    d_send, d_recv,
):
    s = lax.axis_index("section")
    p = lax.axis_index("patch")
    z = p // 4
    xl = (p // 2) % 2
    core = p % 2
    me = z * 2 + core
    after = (s + 1) % NS
    before = (s + NS - 1) % NS
    core_mate = z * 4 + xl * 2 + (1 - core)
    x_mate = z * 4 + (1 - xl) * 2 + core

    def on_line(zs, c):
        return zs * 4 + xl * 2 + c

    loads = [
        pltpu.make_async_copy(x_hbm, x_in, load_sem.at[0]),
        pltpu.make_async_copy(st_hbm.at[s], st_in.at[0], load_sem.at[1]),
        pltpu.make_async_copy(st_hbm.at[before], st_in.at[1], load_sem.at[2]),
        pltpu.make_async_copy(wq_hbm, wq.at[xl], load_sem.at[3]),
        pltpu.make_async_copy(wo_hbm, wo.at[xl], load_sem.at[4]),
        pltpu.make_async_copy(mod_hbm, mod, load_sem.at[5]),
    ]
    for load in loads:
        load.start()

    barrier = pltpu.get_barrier_semaphore()

    def greet(sec, dev):
        pl.semaphore_signal(barrier, inc=1, device_id=(sec, dev), device_id_type=MESH)

    for far in range(1, REACH + 1):
        greet(s, on_line((z + far) % NZ, core))
        greet(s, on_line((z + NZ - far) % NZ, core))
    greet(s, core_mate)
    greet(s, x_mate)
    greet(after, p)
    greet(before, p)

    loads[0].wait()
    xf = x_in[...].astype(F32)
    for t in range(2):
        for k in range(KC):
            rows_f[pl.ds(t * KC + k, 1), :] = xf[t : t + 1, k * 128 : (k + 1) * 128]
    own = pl.ds(pl.multiple_of(me * BLK, 16), BLK)
    g0[own, :] = rows_f[...].astype(BF16)
    def block(g, b):
        return g.at[pl.ds(pl.multiple_of(b * BLK, 16), BLK)]

    def push(src, dst, send, recv, sec, dev):
        pltpu.make_async_remote_copy(
            src_ref=src, dst_ref=dst, send_sem=send, recv_sem=recv,
            device_id=(sec, dev), device_id_type=MESH,
        ).start()

    def take(ref, sem):
        pltpu.make_async_copy(ref, ref, sem).wait()

    my_pair = jnp.int32(0)
    owned = jnp.int32(0)
    for pair in range(PAIRS):
        hit = jnp.where(p == owner_of(pair, xl), 1, 0)
        my_pair = my_pair + pair * hit
        owned = owned + hit

    def finish(stage):
        if stage == 1:
            for load in loads[1:]:
                load.wait()
        if stage == 2:
            @pl.when(owned == 1)
            def _():
                take(stale, st_recv)
        if 2 <= stage < 5:
            pl.semaphore_wait(nready, 1)
        if stage >= 2:
            take(g0.at[pl.ds(0, 31 * BLK)], ag_send.at[0])
            take(wq.at[xl], w_send.at[0])
            take(st_src.at[0], w_send.at[1])
            take(wo.at[xl], w_send.at[2])

            def drain_stale(i, _):
                take(st_src.at[0, pl.ds(0, 16)], st_send)
                return 0

            lax.fori_loop(0, 2 * (PAIRS - owned), drain_stale, 0)
        if 2 <= stage < 4:
            take(wo.at[1 - xl], w_recv.at[2])
        if stage >= 5:
            take(g1, ag_send.at[1])
        if stage >= 8:
            take(dsrc, d_send)
        mine_units = jnp.int32(0)
        for j in range(2):
            for i in range(9):
                unit = (z * 4 + 2 * j + core) * 9 + i
                pair = ((unit // 16) % HEADS) // 2
                mine_units = mine_units + jnp.where(owner_of(pair, xl) == p, 1, 0)
        for tick in range(2):
            def drain(i, _):
                take(qsrc.at[tick, 0, pl.ds(0, 8)], q_send.at[tick])
                return 0

            if stage >= 3 + 3 * tick:
                lax.fori_loop(0, 18 - mine_units, drain, 0)
            if stage >= 4 + 3 * tick:
                def drain_piece(i, _):
                    take(att.at[tick, pl.ds(0, 128)], at_send.at[tick])
                    return 0

                lax.fori_loop(0, 3 + (NZ - 1) * owned, drain_piece, 0)

    def relay_core(g, tick, zs):
        b = zs * 2 + core
        push(block(g, b), block(g, b), ag_send.at[tick], ag_core.at[tick], s, core_mate)

    def arrive(g, tick, i):
        far = (i + 1) // 2
        zs = (z + NZ - far * (2 * (i % 2) - 1)) % NZ
        take(block(g, zs * 2 + core), ag_own.at[tick, zs])
        return zs

    def near_step(g, tick):
        def step(i, _):
            relay_core(g, tick, arrive(g, tick, i))
            return 0

        return step

    def relay(g, tick, first):
        lax.fori_loop(first, 2 * REACH - 1, near_step(g, tick), 0)
        for i in (2 * REACH - 1, 2 * REACH):
            zs = arrive(g, tick, i)
            sign = 2 * (i % 2) - 1
            piece = block(g, zs * 2 + core)
            for far in range(REACH - 1 + i % 2, 0, -1):
                dev = on_line((z + NZ + sign * far) % NZ, core)
                push(piece, piece, ag_send.at[tick], ag_own.at[tick, zs], s, dev)
            relay_core(g, tick, zs)
        lax.fori_loop(2 * REACH + 1, NZ, near_step(g, tick), 0)
        take(g.at[pl.ds(0, NZ * BLK)], ag_core.at[tick])

    def spread(src, dst, tick, sec, first):
        def send(far, sign):
            dev = on_line((z + NZ + sign * far) % NZ, core)
            push(src, dst, ag_send.at[tick], ag_own.at[tick, z], sec, dev)

        send(REACH, 1)
        send(REACH, -1)
        if first == 0:
            send(0, 1)
        for far in range(1, REACH):
            send(far, 1)
            send(far, -1)

    pl.semaphore_wait(barrier, 2 * REACH + 4)

    spread(g0.at[own], g0.at[own], 0, s, 1)
    relay_core(g0, 0, z)
    loads[3].wait()
    push(wq.at[xl], wq.at[xl], w_send.at[0], w_recv.at[0], s, x_mate)
    loads[1].wait()
    loads[2].wait()
    for tick in range(2):
        sf = st_in[tick].astype(F32)
        for kv in range(2):
            for head in range(HEADS):
                for t in range(2):
                    row = (head // 2) * 16 + (((head % 2) * 2 + tick) * 2 + kv) * 2 + t
                    low = (kv * HEADS + head) * 128
                    gran_f[pl.ds(row, 1), :] = sf[t : t + 1, low : low + 128]
    st_src[0] = gran_f[...].astype(BF16)
    push(st_src.at[0], st_src.at[1], w_send.at[1], w_recv.at[1], s, x_mate)
    loads[4].wait()
    push(wo.at[xl], wo.at[xl], w_send.at[2], w_recv.at[2], s, x_mate)
    loads[5].wait()


    times = [time_ref[s], time_ref[before]]
    lane = lax.broadcasted_iota(jnp.int32, (128, 128), 1)
    first_half = lane < 64

    def fold(tick, j):
        shift_sum = jnp.zeros((QROWS, 128), F32)
        row_sum = jnp.zeros((QROWS, 128), F32)
        base = times[tick] * 3
        for k in range(KC):
            lanes = pl.ds(k * 128, 128)
            shift = mod[base, :, lanes]
            scale = mod[base + 1, :, lanes]
            w = wq[j, :, lanes].astype(F32)
            scaled = (w * (1.0 + scale)).astype(BF16)
            wmod[tick, j, :, lanes] = scaled
            shift_sum += w * shift
            row_sum += scaled.astype(F32)
        for n, value in enumerate((shift_sum, row_sum)):
            total = jnp.sum(value, axis=1, keepdims=True)
            colv[tick, n, j] = jnp.broadcast_to(total, (QROWS, 128))

    fold(0, xl)

    feature = lax.broadcasted_iota(jnp.int32, (BLK, 128), 1)
    row = lax.broadcasted_iota(jnp.int32, (BLK, 128), 0)
    gate_sums = []
    for j in range(2):
        mine = (z * 4 + 2 * j + core) * BLK + row
        sums = [jnp.zeros((BLK, 128), F32), jnp.zeros((BLK, 128), F32)]
        for k in range(KC):
            lanes = pl.ds(k * 128, 128)
            here = feature + k * 128 == mine
            pick[j, :, lanes] = jnp.where(here, 1.0, 0.0).astype(BF16)
            for tick in range(2):
                sums[tick] += jnp.where(here, mod[times[tick] * 3 + 2, :, lanes], 0.0)
        gate_sums.append([jnp.sum(v, axis=1, keepdims=True) for v in sums])
    for tick in range(2):
        gatev[tick] = jnp.where(first_half[:BLK], gate_sums[0][tick], gate_sums[1][tick])

    @pl.when(owned == 1)
    def _():
        r = lax.broadcasted_iota(jnp.int32, (128, 128), 0)
        for j, ref in enumerate((qg_ref, kg_ref)):
            diag = jnp.where(r == lane, jnp.broadcast_to(ref[...], (128, 128)), 0.0)
            gains[j] = jnp.broadcast_to(jnp.sum(diag, axis=1, keepdims=True), (128, 128))
        pr = r[:64]
        pc = lane[:64]
        places = jnp.broadcast_to(order_ref[...].astype(F32), (64, 64))
        column = jnp.sum(
            jnp.where(pr[:, :64] == pc[:, :64], places, 0.0), axis=1, keepdims=True
        )
        token = pc % 64
        patch = ((token % LINE) // 2) * 4 + 2 * xl + token % 2
        place = jnp.sum(jnp.where(pr == patch, column, 0.0), axis=0, keepdims=True)
        pos = place * 2.0 + jnp.where(token[:1] < LINE, 0.0, 1.0)
        freq = jnp.exp(pr.astype(F32) * (-jnp.log(F32(10000.0)) / 64.0))
        angle = pos * freq
        table[0] = jnp.cos(angle)
        table[1] = jnp.sin(angle)

    relay(g0, 0, 1)
    pl.semaphore_signal(nready, inc=1, device_id=(before, p), device_id_type=MESH)

    take(st_src.at[1], w_recv.at[1])
    for pair in range(PAIRS):
        dev = owner_of(pair, xl)
        for j in range(2):
            src = st_src.at[j, pl.ds(pair * 16, 16)]
            origin = z * 4 + 2 * (xl if j == 0 else 1 - xl) + core
            dst = stale.at[pl.ds(pl.multiple_of(origin * 16, 16), 16)]

            @pl.when(p == dev)
            def _():
                pltpu.make_async_copy(src, dst, st_recv).start()

            @pl.when(p != dev)
            def _():
                push(src, dst, st_send, st_recv, s, dev)

    take(wq.at[1 - xl], w_recv.at[0])
    fold(0, 1 - xl)

    def send_qkv(tick):
        for j in range(2):
            for i in range(9):
                unit = (z * 4 + 2 * j + core) * 9 + i
                part = unit // 16
                head = part % HEADS
                dev = owner_of(head // 2, xl)
                kind = part // HEADS
                low = pl.multiple_of(kind * 128 + (unit % 16) * 8, 8)
                src = qsrc.at[tick, j, pl.ds(i * 8, 8)]
                dst = qrecv.at[tick, head % 2, pl.ds(low, 8)]

                @pl.when(p == dev)
                def _():
                    pltpu.make_async_copy(src, dst, q_recv.at[tick]).start()

                @pl.when(p != dev)
                def _():
                    push(src, dst, q_send.at[tick], q_recv.at[tick], s, dev)

    def finish_qkv(tick, accs, mean, var):
        rstd = lax.rsqrt(var + 1e-06)
        for j in range(2):
            qkv = rstd * (accs[j] - colv[tick, 1, j] * mean) + colv[tick, 0, j]
            qsrc[tick, j] = qkv.astype(BF16).astype(F32)

    for b in range(12):
        part = pl.ds(b * 128, 128)
        wide[part, :] = g0[part, :].astype(F32)
    total = jnp.zeros((64, 128), F32)
    for k in range(KC):
        lanes = pl.ds(k * 128, 128)
        piece = jnp.concatenate(
            [wide[pl.ds(t * KC + k, LINE, stride=BLK), :] for t in range(2)], axis=0
        )
        total += piece
        narrow = piece.astype(BF16)
        xr[pl.ds(0, 64), lanes] = narrow
        xr[pl.ds(64, 64), lanes] = narrow
    accs = [dot_nt(wmod[0, j], xr[...]) for j in range(2)]
    mean_c = jnp.sum(total, axis=1, keepdims=True) * (1.0 / D)
    total = jnp.zeros((64, 128), F32)
    for k in range(KC):
        centred = xr[pl.ds(0, 64), pl.ds(k * 128, 128)].astype(F32) - mean_c
        total += centred * centred
    var_c = jnp.sum(total, axis=1, keepdims=True) * (1.0 / D)
    stats = jnp.where(first_half[:64], mean_c, var_c)
    stats = jnp.transpose(jnp.concatenate([stats, stats], axis=0))
    finish_qkv(0, accs, stats[0:1, :], stats[64:65, :])
    send_qkv(0)

    @pl.when(owned == 1)
    def _():
        take(stale, st_recv)
        for b in range(8):
            part = pl.ds(b * 128, 128)
            stale_f[part, :] = stale[part, :].astype(F32)
        for tick in range(2):
            for second in range(2):
                got = []
                for kv in range(2):
                    both = [
                        stale_f[
                            pl.ds(((second * 2 + tick) * 2 + kv) * 2 + t, 64, stride=16), :
                        ]
                        for t in range(2)
                    ]
                    got.append(jnp.concatenate(both, axis=0))
                keys[tick, second] = got[0].astype(BF16)
                vals[tick, second] = jnp.transpose(got[1]).astype(BF16)

    def attend(tick):
        take(qrecv.at[tick], q_recv.at[tick])
        factor = 128.0 ** -0.5
        cosine, sine = table[0], table[1]

        def received(low):
            part = pl.ds(low, 128)
            return jnp.where(first_half, qrecv[tick, 0, part, :], qrecv[tick, 1, part, :])

        def prepared(low, j):
            u = received(low)
            square = jnp.sum(u * u, axis=0, keepdims=True) * (1.0 / 128)
            u = u * lax.rsqrt(square + 1e-06) * gains[j]
            a, b = u[:64], u[64:]
            return jnp.concatenate(
                [a * cosine - b * sine, a * sine + b * cosine], axis=0
            ).astype(BF16)

        def partner(u):
            up = pltpu.roll(u, 128 - LINE, 1)
            down = pltpu.roll(u, LINE, 1)
            return jnp.where(lane % 64 < LINE, up, down)

        query = prepared(0, 0)
        key = prepared(128, 1).astype(F32)
        value = received(256)
        scores = jnp.where(
            first_half, dot_nn(keys[tick, 0], query), dot_nn(keys[tick, 1], query)
        ) * factor
        r = lax.broadcasted_iota(jnp.int32, (128, 128), 0)
        patch = ((lane % LINE) // 2) * 4 + 2 * xl + lane % 2
        scores = jnp.where(r % 64 == patch, -1e30, scores)
        wide_q = query.astype(F32)
        same = jnp.sum(wide_q * key, axis=0, keepdims=True) * factor
        other = jnp.sum(wide_q * partner(key), axis=0, keepdims=True) * factor
        top = jnp.maximum(jnp.max(scores, axis=0, keepdims=True), jnp.maximum(same, other))
        weights = jnp.exp(scores - top)
        same = jnp.exp(same - top)
        other = jnp.exp(other - top)
        mass = jnp.sum(weights, axis=0, keepdims=True) + same + other
        weights = weights.astype(BF16)
        summed = jnp.where(
            first_half, dot_nn(vals[tick, 0], weights), dot_nn(vals[tick, 1], weights)
        )
        summed = summed + same * value + other * partner(value)
        att[tick, pair_rows(my_pair), :] = (summed / mass).astype(BF16)

    def pair_rows(pair):
        return pl.ds(pl.multiple_of(pair * 128, 128), 128)

    def send_attended(tick):
        piece = att.at[tick, pair_rows(my_pair)]

        def send(i, _):
            far = (NZ - i + 1) // 2
            dev = on_line((z + NZ + far * (2 * (i % 2) - 1)) % NZ, core)
            push(piece, piece, at_send.at[tick], at_own.at[tick, my_pair // 2], s, dev)
            return 0

        lax.fori_loop(1, NZ, send, 0)

    def gather_attended(tick):
        for j in range(3):
            pair = j * 2 + core
            piece = att.at[tick, pair_rows(pair)]

            @pl.when(owner_of(pair, xl) != p)
            def _():
                take(piece, at_own.at[tick, j])

            push(piece, piece, at_send.at[tick], at_core.at[tick], s, core_mate)
        take(att.at[tick, pl.ds(0, 3 * 128)], at_core.at[tick])

    def project(tick, residual):
        out = jnp.where(
            first_half[: 2 * BLK], dot_nn(weven[...], att[tick]), dot_nn(wodd[...], att[tick])
        )
        out = out + pltpu.roll(out, 64, 1)
        out = jnp.where(first_half[:BLK], out[:BLK], out[BLK:])
        return (residual + gatev[tick] * out).astype(BF16)

    @pl.when(owned == 1)
    def _():
        attend(0)

    @pl.when(owned == 1)
    def _():
        send_attended(0)

    picked = [dot_nt(pick[j], xr[...]) for j in range(2)]
    residual = jnp.where(first_half[:BLK], picked[0], picked[1])
    take(wo.at[1 - xl], w_recv.at[2])
    for j in range(2):
        for pair in range(PAIRS):
            at = pl.ds(j * BLK, BLK), pl.ds(pair * 128, 128)
            weven[at] = wo[j, :, pl.ds(pair * 256, 128)]
            wodd[at] = wo[j, :, pl.ds(pair * 256 + 128, 128)]
    pf = lax.broadcasted_iota(jnp.int32, (CHUNK, 128), 0)
    po = lax.broadcasted_iota(jnp.int32, (CHUNK, 128), 1)
    for k in range(CHUNK // 128):
        to = po + (k % 3) * 128
        group = jnp.where(to >= 96, 1, 0) + jnp.where(to >= 192, 1, 0) + jnp.where(to >= 288, 1, 0)
        source = to + 96 * group + 96 * (k // 3)
        perm[:, pl.ds(k * 128, 128)] = jnp.where(pf == source, 1.0, 0.0).astype(BF16)
    half = CHUNK // 2
    for j in range(2):
        fold(1, j)
        for k in range(D // CHUNK):
            moved = dot_nn(wmod[1, j, :, pl.ds(k * CHUNK, CHUNK)], perm[...]).astype(BF16)
            wlow[j, :, pl.ds(k * half, half)] = moved[:, :half]
            whigh[j, :, pl.ds(k * half, half)] = moved[:, half:]

    gather_attended(0)
    ysrc[...] = project(0, residual)

    pl.semaphore_wait(nready, 1)
    spread(ysrc, g1.at[own], 1, after, 0)

    relay(g1, 1, 0)
    accs = []
    for j in range(2):
        acc = jnp.where(
            first_half[:QROWS], dot_nn(wlow[j], g1[...]), dot_nn(whigh[j], g1[...])
        )
        accs.append(acc + pltpu.roll(acc, 64, 1))
    total = jnp.zeros((128, 128), F32)
    for k in range(12):
        total += g1[pl.ds(k * 128, 128), :].astype(F32)
    total = jnp.sum(total, axis=0, keepdims=True)
    mean = (total + pltpu.roll(total, 64, 1)) * (1.0 / D)
    total = jnp.zeros((128, 128), F32)
    for k in range(12):
        centred = g1[pl.ds(k * 128, 128), :].astype(F32) - mean
        total += centred * centred
    total = jnp.sum(total, axis=0, keepdims=True)
    var = (total + pltpu.roll(total, 64, 1)) * (1.0 / D)
    finish_qkv(1, accs, mean, var)
    send_qkv(1)

    @pl.when(owned == 1)
    def _():
        attend(1)

    @pl.when(owned == 1)
    def _():
        send_attended(1)

    gather_attended(1)
    last = project(1, g1[own, :].astype(F32)).astype(F32)
    blank = jnp.zeros((16, 128), F32)
    turned = jnp.transpose(
        jnp.concatenate([last, blank, pltpu.roll(last, 64, 1), blank], axis=0)
    )
    for i in range(LINE):
        for t in range(2):
            dsrc[i, pl.ds(t, 1), :] = turned[t * LINE + i : t * LINE + i + 1, :]

    def last_send(i, _):
        to = (me + i) % LINE
        push(dsrc.at[to], drecv.at[me], d_send, d_recv, after, on_line(to // 2, to % 2))
        return 0

    lax.fori_loop(0, LINE, last_send, 0)
    take(drecv, d_recv)
    out_ref[...] = drecv[...]
    finish(8)


def per_device(states, w_qkv, w_out, mod_table, q_gain, k_gain, stale_kv, timestep, patch_order):
    hbm = pl.BlockSpec(memory_space=pl.ANY)
    vmem = pl.BlockSpec(memory_space=pltpu.VMEM)
    dma = pltpu.SemaphoreType.DMA
    regular = pltpu.SemaphoreType.REGULAR
    got = pl.pallas_call(
        kernel,
        out_shape=jax.ShapeDtypeStruct((LINE, 2, 128), F32),
        in_specs=[hbm] * 5 + [vmem] * 3 + [pl.BlockSpec(memory_space=pltpu.SMEM)],
        out_specs=vmem,
        scratch_shapes=[
            pltpu.VMEM((2, D), BF16),
            pltpu.VMEM((2, QROWS, D), BF16),
            pltpu.VMEM((2, BLK, D // 2), BF16),
            pltpu.VMEM((84, 1, D), F32),
            pltpu.VMEM((2, 2, D), BF16),
            pltpu.VMEM((BLK, 128), F32),
            pltpu.VMEM((2, 96, 128), BF16),
            pltpu.VMEM((96, 128), F32),
            pltpu.VMEM((LINE * BLK, 128), BF16),
            pltpu.VMEM((LINE * BLK, 128), BF16),
            pltpu.VMEM((LINE * BLK, 128), F32),
            pltpu.VMEM((128, D), BF16),
            pltpu.VMEM((2, 2, QROWS, D), BF16),
            pltpu.VMEM((2 * BLK, D // 4), BF16),
            pltpu.VMEM((2 * BLK, D // 4), BF16),
            pltpu.VMEM((CHUNK, CHUNK), BF16),
            pltpu.VMEM((2, QROWS, D // 2), BF16),
            pltpu.VMEM((2, QROWS, D // 2), BF16),
            pltpu.VMEM((2, BLK, D), BF16),
            pltpu.VMEM((2, 2, 2, QROWS, 128), F32),
            pltpu.VMEM((2, BLK, 128), F32),
            pltpu.VMEM((2, 64, 128), F32),
            pltpu.VMEM((2, 128, 128), F32),
            pltpu.VMEM((2, 2, QROWS, 128), F32),
            pltpu.VMEM((2, 2, 384, 128), F32),
            pltpu.VMEM((1024, 128), BF16),
            pltpu.VMEM((1024, 128), F32),
            pltpu.VMEM((2, 2, 128, 128), BF16),
            pltpu.VMEM((2, 2, 128, 128), BF16),
            pltpu.VMEM((2, PAIRS * 128, 128), BF16),
            pltpu.VMEM((BLK, 128), BF16),
            pltpu.VMEM((LINE, 2, 128), F32),
            pltpu.VMEM((LINE, 2, 128), F32),
            dma((6,)),
            regular,
            dma((3,)),
            dma((3,)),
            dma((2,)),
            dma((2, NZ)),
            dma((2,)),
            dma,
            dma,
            dma((2,)),
            dma((2,)),
            dma((2,)),
            dma((2, 3)),
            dma((2,)),
            dma,
            dma,
        ],
        compiler_params=pltpu.CompilerParams(
            collective_id=0, has_side_effects=True, vmem_limit_bytes=56 * 2**20
        ),
        name="block_cycle",
    )(
        states[0],
        w_qkv[0].T,
        w_out[0].T,
        jnp.transpose(mod_table, (0, 2, 1, 3)).reshape(84, 1, D),
        stale_kv[0],
        patch_order.reshape(1, 64),
        q_gain,
        k_gain,
        timestep,
    )
    split = got.reshape(NZ, 2, 2, 2, 64)[..., :BLK]
    return jnp.transpose(split, (2, 0, 3, 1, 4)).reshape(1, 2, D).astype(BF16)


def solution(mesh):
    in_specs = (
        P("section", "patch", None),
        P("section", None, "patch"),
        P("section", None, "patch"),
        P(None, "section", None, None),
        P("section", None),
        P("section", None),
        P("section", None, "patch", None),
        P(),
        P(),
    )
    out_specs = P("section", "patch", None)
    return jax.shard_map(
        per_device, mesh=mesh, in_specs=in_specs, out_specs=out_specs, check_vma=False
    )
```

```python
import jax
import jax.numpy as jnp
from jax import lax
from jax.experimental import pallas as pl
from jax.experimental.pallas import tpu as pltpu
from jax.sharding import PartitionSpec as P

MESH = pl.DeviceIdType.MESH
F32 = jnp.float32
BF16 = jnp.bfloat16
NZ = 16
NS = 8
BLK = 48
HEADS = 12
PAIRS = 6
D = 3072
KC = D // 128
LINE = 32
QROWS = 72
REACH = 4
CHUNK = 768


def owner_of(pair, line):
    part = ((pair + line) % 3) * PAIRS + pair
    centre = (32 * part + 16) // 9
    return (centre // 4) * 4 + 2 * line + pair % 2


def dot_nt(a, b):
    return lax.dot_general(a, b, (((1,), (1,)), ((), ())), preferred_element_type=F32)


def dot_nn(a, b):
    return lax.dot_general(a, b, (((1,), (0,)), ((), ())), preferred_element_type=F32)


def kernel(
    x_hbm, wq_hbm, wo_hbm, mod_hbm, st_hbm, order_ref, qg_ref, kg_ref, time_ref,
    out_ref,
    x_in, wq, wo, mod, st_in, rows_f, st_src, st_own, st_mate, gran_f,
    g0, g1, wide, xr, wmod, wodd, weven, perm, wlow, whigh, pick, colv, gatev, table, gains,
    qsrc, qrecv, merged, stale, stale_f, keys, vals, att, ysrc, dsrc, drecv,
    load_sem, nready, w_send, w_recv,
    ag_send, ag_own, ag_core,
    st_send, st_recv, q_send, q_recv,
    at_send, at_own, at_core,
    d_send, d_recv,
):
    s = lax.axis_index("section")
    p = lax.axis_index("patch")
    z = p // 4
    xl = (p // 2) % 2
    core = p % 2
    me = z * 2 + core
    after = (s + 1) % NS
    before = (s + NS - 1) % NS
    core_mate = z * 4 + xl * 2 + (1 - core)
    x_mate = z * 4 + (1 - xl) * 2 + core

    def on_line(zs, c):
        return zs * 4 + xl * 2 + c

    loads = [
        pltpu.make_async_copy(x_hbm, x_in, load_sem.at[0]),
        pltpu.make_async_copy(st_hbm.at[s], st_in.at[0], load_sem.at[1]),
        pltpu.make_async_copy(st_hbm.at[before], st_in.at[1], load_sem.at[2]),
        pltpu.make_async_copy(wq_hbm, wq.at[xl], load_sem.at[3]),
        pltpu.make_async_copy(wo_hbm, wo.at[xl], load_sem.at[4]),
        pltpu.make_async_copy(mod_hbm, mod, load_sem.at[5]),
    ]
    for load in loads:
        load.start()

    barrier = pltpu.get_barrier_semaphore()

    def greet(sec, dev):
        pl.semaphore_signal(barrier, inc=1, device_id=(sec, dev), device_id_type=MESH)

    for far in range(1, REACH + 1):
        greet(s, on_line((z + far) % NZ, core))
        greet(s, on_line((z + NZ - far) % NZ, core))
    greet(s, core_mate)
    greet(s, x_mate)
    greet(after, p)
    greet(before, p)

    loads[0].wait()
    xf = x_in[...].astype(F32)
    for t in range(2):
        for k in range(KC):
            rows_f[pl.ds(t * KC + k, 1), :] = xf[t : t + 1, k * 128 : (k + 1) * 128]
    own = pl.ds(pl.multiple_of(me * BLK, 16), BLK)
    g0[own, :] = rows_f[...].astype(BF16)
    def block(g, b):
        return g.at[pl.ds(pl.multiple_of(b * BLK, 16), BLK)]

    def push(src, dst, send, recv, sec, dev):
        pltpu.make_async_remote_copy(
            src_ref=src, dst_ref=dst, send_sem=send, recv_sem=recv,
            device_id=(sec, dev), device_id_type=MESH,
        ).start()

    def take(ref, sem):
        pltpu.make_async_copy(ref, ref, sem).wait()

    my_pair = jnp.int32(0)
    owned = jnp.int32(0)
    for pair in range(PAIRS):
        hit = jnp.where(p == owner_of(pair, xl), 1, 0)
        my_pair = my_pair + pair * hit
        owned = owned + hit

    def drain_stale(tick):
        def step(i, _):
            take(st_src.at[tick, pl.ds(0, 16)], st_send.at[tick])
            return 0

        lax.fori_loop(0, PAIRS - owned, step, 0)

    def finish(stage):
        if stage == 1:
            for load in loads[1:]:
                load.wait()
        if stage == 2:
            @pl.when(owned == 1)
            def _():
                take(stale.at[0], st_recv.at[0])
            take(wq.at[1 - xl], w_recv.at[0])
        if 3 <= stage < 6:
            @pl.when(owned == 1)
            def _():
                take(stale.at[1], st_recv.at[1])
        if 2 <= stage < 5:
            pl.semaphore_wait(nready, 1)
        if stage >= 2:
            take(g0.at[pl.ds(0, 31 * BLK)], ag_send.at[0])
            take(wq.at[xl], w_send.at[0])
            take(wo.at[xl], w_send.at[2])

            drain_stale(0)
            take(st_own, w_send.at[1])
        if 2 <= stage < 4:
            take(wo.at[1 - xl], w_recv.at[2])
        if stage >= 3:
            drain_stale(1)
        if stage >= 5:
            take(g1, ag_send.at[1])
        if stage >= 8:
            take(dsrc, d_send)
        mine_units = jnp.int32(0)
        for j in range(2):
            for i in range(9):
                unit = (z * 4 + 2 * j + core) * 9 + i
                pair = ((unit // 16) % HEADS) // 2
                mine_units = mine_units + jnp.where(owner_of(pair, xl) == p, 1, 0)
        for tick in range(2):
            def drain(i, _):
                take(qsrc.at[tick, 0, 0], q_send.at[tick])
                return 0

            if stage >= 3 + 3 * tick:
                lax.fori_loop(0, 18 - mine_units, drain, 0)
            if stage >= 4 + 3 * tick:
                def drain_piece(i, _):
                    take(att.at[tick, pl.ds(0, 128)], at_send.at[tick])
                    return 0

                lax.fori_loop(0, 3 + (NZ - 1) * owned, drain_piece, 0)

    def relay_core(g, tick, zs):
        b = zs * 2 + core
        push(block(g, b), block(g, b), ag_send.at[tick], ag_core.at[tick], s, core_mate)

    def arrive(g, tick, i):
        far = (i + 1) // 2
        zs = (z + NZ - far * (2 * (i % 2) - 1)) % NZ
        take(block(g, zs * 2 + core), ag_own.at[tick, zs])
        return zs

    def near_step(g, tick):
        def step(i, _):
            relay_core(g, tick, arrive(g, tick, i))
            return 0

        return step

    def relay(g, tick, first):
        lax.fori_loop(first, 2 * REACH - 1, near_step(g, tick), 0)
        for i in (2 * REACH - 1, 2 * REACH):
            zs = arrive(g, tick, i)
            sign = 2 * (i % 2) - 1
            piece = block(g, zs * 2 + core)
            for far in range(REACH - 1 + i % 2, 0, -1):
                dev = on_line((z + NZ + sign * far) % NZ, core)
                push(piece, piece, ag_send.at[tick], ag_own.at[tick, zs], s, dev)
            relay_core(g, tick, zs)
        lax.fori_loop(2 * REACH + 1, NZ, near_step(g, tick), 0)
        take(g.at[pl.ds(0, NZ * BLK)], ag_core.at[tick])

    def spread(src, dst, tick, sec, first):
        def send(far, sign):
            dev = on_line((z + NZ + sign * far) % NZ, core)
            push(src, dst, ag_send.at[tick], ag_own.at[tick, z], sec, dev)

        send(REACH, 1)
        send(REACH, -1)
        if first == 0:
            send(0, 1)
        for far in range(1, REACH):
            send(far, 1)
            send(far, -1)

    pl.semaphore_wait(barrier, 2 * REACH + 4)

    spread(g0.at[own], g0.at[own], 0, s, 1)
    relay_core(g0, 0, z)
    loads[3].wait()
    push(wq.at[xl], wq.at[xl], w_send.at[0], w_recv.at[0], s, x_mate)
    loads[1].wait()
    loads[2].wait()
    for tick in range(2):
        sf = st_in[tick].astype(F32)
        for kv in range(2):
            for head in range(HEADS):
                for t in range(2):
                    row = tick * 48 + (head // 2) * 8 + ((head % 2) * 2 + kv) * 2 + t
                    low = (kv * HEADS + head) * 128
                    gran_f[pl.ds(row, 1), :] = sf[t : t + 1, low : low + 128]
    st_own[...] = gran_f[...].astype(BF16)
    push(st_own, st_mate, w_send.at[1], w_recv.at[1], s, x_mate)
    loads[4].wait()
    push(wo.at[xl], wo.at[xl], w_send.at[2], w_recv.at[2], s, x_mate)
    loads[5].wait()


    times = [time_ref[s], time_ref[before]]
    lane = lax.broadcasted_iota(jnp.int32, (128, 128), 1)
    first_half = lane < 64

    def fold(tick, j):
        shift_sum = jnp.zeros((QROWS, 128), F32)
        row_sum = jnp.zeros((QROWS, 128), F32)
        base = times[tick] * 3
        for k in range(KC):
            lanes = pl.ds(k * 128, 128)
            shift = mod[base, :, lanes]
            scale = mod[base + 1, :, lanes]
            w = wq[j, :, lanes].astype(F32)
            scaled = (w * (1.0 + scale)).astype(BF16)
            wmod[tick, j, :, lanes] = scaled
            shift_sum += w * shift
            row_sum += scaled.astype(F32)
        for n, value in enumerate((shift_sum, row_sum)):
            total = jnp.sum(value, axis=1, keepdims=True)
            colv[tick, n, j] = jnp.broadcast_to(total, (QROWS, 128))

    fold(0, xl)

    feature = lax.broadcasted_iota(jnp.int32, (BLK, 128), 1)
    row = lax.broadcasted_iota(jnp.int32, (BLK, 128), 0)
    gate_sums = []
    for j in range(2):
        mine = (z * 4 + 2 * j + core) * BLK + row
        sums = [jnp.zeros((BLK, 128), F32), jnp.zeros((BLK, 128), F32)]
        for k in range(KC):
            lanes = pl.ds(k * 128, 128)
            here = feature + k * 128 == mine
            pick[j, :, lanes] = jnp.where(here, 1.0, 0.0).astype(BF16)
            for tick in range(2):
                sums[tick] += jnp.where(here, mod[times[tick] * 3 + 2, :, lanes], 0.0)
        gate_sums.append([jnp.sum(v, axis=1, keepdims=True) for v in sums])
    for tick in range(2):
        gatev[tick] = jnp.where(first_half[:BLK], gate_sums[0][tick], gate_sums[1][tick])

    @pl.when(owned == 1)
    def _():
        r = lax.broadcasted_iota(jnp.int32, (128, 128), 0)
        for j, ref in enumerate((qg_ref, kg_ref)):
            diag = jnp.where(r == lane, jnp.broadcast_to(ref[...], (128, 128)), 0.0)
            gains[j] = jnp.broadcast_to(jnp.sum(diag, axis=1, keepdims=True), (128, 128))
        pr = r[:64]
        pc = lane[:64]
        places = jnp.broadcast_to(order_ref[...].astype(F32), (64, 64))
        column = jnp.sum(
            jnp.where(pr[:, :64] == pc[:, :64], places, 0.0), axis=1, keepdims=True
        )
        token = pc % 64
        patch = ((token % LINE) // 2) * 4 + 2 * xl + token % 2
        place = jnp.sum(jnp.where(pr == patch, column, 0.0), axis=0, keepdims=True)
        pos = place * 2.0 + jnp.where(token[:1] < LINE, 0.0, 1.0)
        freq = jnp.exp(pr.astype(F32) * (-jnp.log(F32(10000.0)) / 64.0))
        angle = pos * freq
        table[0] = jnp.cos(angle)
        table[1] = jnp.sin(angle)

    relay(g0, 0, 1)
    pl.semaphore_signal(nready, inc=1, device_id=(before, p), device_id_type=MESH)

    def send_stale(tick):
        for pair in range(PAIRS):
            dev = owner_of(pair, xl)
            src = st_src.at[tick, pl.ds(pair * 16, 16)]
            dst = stale.at[tick, pl.ds(pl.multiple_of(me * 16, 16), 16)]

            @pl.when(p == dev)
            def _():
                pltpu.make_async_copy(src, dst, st_recv.at[tick]).start()

            @pl.when(p != dev)
            def _():
                push(src, dst, st_send.at[tick], st_recv.at[tick], s, dev)

    take(st_mate, w_recv.at[1])
    other_f = st_mate[...].astype(F32)
    own_f = gran_f[...]
    low_f = jnp.where(xl == 0, own_f, other_f)
    high_f = jnp.where(xl == 0, other_f, own_f)
    for tick in range(2):
        for pair in range(PAIRS):
            low = tick * 48 + pair * 8
            both = jnp.concatenate([low_f[low : low + 8], high_f[low : low + 8]], axis=0)
            st_src[tick, pl.ds(pair * 16, 16), :] = both.astype(BF16)
    send_stale(0)


    def send_qkv(tick, j, acc, mean, var):
        qkv = lax.rsqrt(var + 1e-06) * (acc - colv[tick, 1, j] * mean) + colv[tick, 0, j]
        qkv = qkv.astype(BF16).astype(F32)
        for i in range(9):
            top, bottom = qkv[i * 8 : i * 8 + 4], qkv[i * 8 + 4 : i * 8 + 8]
            qsrc[tick, j, i] = jnp.where(first_half[:4], top, bottom)
        for i in range(9):
            unit = (z * 4 + 2 * j + core) * 9 + i
            part = unit // 16
            head = part % HEADS
            dev = owner_of(head // 2, xl)
            src = qsrc.at[tick, j, i]
            dst = qrecv.at[tick, head % 2, (part // HEADS) * 16 + unit % 16]

            @pl.when(p == dev)
            def _():
                pltpu.make_async_copy(src, dst, q_recv.at[tick]).start()

            @pl.when(p != dev)
            def _():
                push(src, dst, q_send.at[tick], q_recv.at[tick], s, dev)

    for b in range(12):
        part = pl.ds(b * 128, 128)
        wide[part, :] = g0[part, :].astype(F32)
    total = jnp.zeros((64, 128), F32)
    for k in range(KC):
        lanes = pl.ds(k * 128, 128)
        piece = jnp.concatenate(
            [wide[pl.ds(t * KC + k, LINE, stride=BLK), :] for t in range(2)], axis=0
        )
        total += piece
        narrow = piece.astype(BF16)
        xr[pl.ds(0, 64), lanes] = narrow
        xr[pl.ds(64, 64), lanes] = narrow
    acc_own = dot_nt(wmod[0, xl], xr[...])
    mean_c = jnp.sum(total, axis=1, keepdims=True) * (1.0 / D)
    total = jnp.zeros((64, 128), F32)
    for k in range(KC):
        centred = xr[pl.ds(0, 64), pl.ds(k * 128, 128)].astype(F32) - mean_c
        total += centred * centred
    var_c = jnp.sum(total, axis=1, keepdims=True) * (1.0 / D)
    stats = jnp.where(first_half[:64], mean_c, var_c)
    stats = jnp.transpose(jnp.concatenate([stats, stats], axis=0))
    mean0, var0 = stats[0:1, :], stats[64:65, :]
    send_qkv(0, xl, acc_own, mean0, var0)
    take(wq.at[1 - xl], w_recv.at[0])
    fold(0, 1 - xl)
    send_qkv(0, 1 - xl, dot_nt(wmod[0, 1 - xl], xr[...]), mean0, var0)
    send_stale(1)

    def unpack_stale(tick):
        take(stale.at[tick], st_recv.at[tick])
        for b in range(4):
            part = pl.ds(b * 128, 128)
            stale_f[part, :] = stale[tick, part, :].astype(F32)
        for second in range(2):
            got = []
            for kv in range(2):
                pieces = [
                    stale_f[pl.ds(line * 8 + (second * 2 + kv) * 2 + t, LINE, stride=16), :]
                    for t in range(2)
                    for line in range(2)
                ]
                got.append(jnp.concatenate(pieces, axis=0))
            keys[tick, second] = got[0].astype(BF16)
            vals[tick, second] = jnp.transpose(got[1]).astype(BF16)

    @pl.when(owned == 1)
    def _():
        unpack_stale(0)

    def attend(tick):
        take(qrecv.at[tick], q_recv.at[tick])
        factor = 128.0 ** -0.5
        cosine, sine = table[0], table[1]

        def received(kind):
            left = first_half[:4]
            for i in range(16):
                first, second = qrecv[tick, 0, kind * 16 + i], qrecv[tick, 1, kind * 16 + i]
                merged[kind, pl.ds(i * 8, 4), :] = jnp.where(
                    left, first, pltpu.roll(second, 64, 1)
                )
                merged[kind, pl.ds(i * 8 + 4, 4), :] = jnp.where(
                    left, pltpu.roll(first, 64, 1), second
                )
            return merged[kind]

        def prepared(j):
            u = received(j)
            square = jnp.sum(u * u, axis=0, keepdims=True) * (1.0 / 128)
            u = u * lax.rsqrt(square + 1e-06) * gains[j]
            a, b = u[:64], u[64:]
            return jnp.concatenate(
                [a * cosine - b * sine, a * sine + b * cosine], axis=0
            ).astype(BF16)

        def partner(u):
            up = pltpu.roll(u, 128 - LINE, 1)
            down = pltpu.roll(u, LINE, 1)
            return jnp.where(lane % 64 < LINE, up, down)

        query = prepared(0)
        key = prepared(1).astype(F32)
        value = received(2)
        scores = jnp.where(
            first_half, dot_nn(keys[tick, 0], query), dot_nn(keys[tick, 1], query)
        ) * factor
        r = lax.broadcasted_iota(jnp.int32, (128, 128), 0)
        key_line = (r // LINE) % 2
        own_patch = (r % LINE == lane % LINE) & (key_line == xl)
        scores = jnp.where(own_patch, -1e30, scores)
        wide_q = query.astype(F32)
        same = jnp.sum(wide_q * key, axis=0, keepdims=True) * factor
        other = jnp.sum(wide_q * partner(key), axis=0, keepdims=True) * factor
        top = jnp.maximum(jnp.max(scores, axis=0, keepdims=True), jnp.maximum(same, other))
        weights = jnp.exp(scores - top)
        same = jnp.exp(same - top)
        other = jnp.exp(other - top)
        mass = jnp.sum(weights, axis=0, keepdims=True) + same + other
        weights = weights.astype(BF16)
        summed = jnp.where(
            first_half, dot_nn(vals[tick, 0], weights), dot_nn(vals[tick, 1], weights)
        )
        summed = summed + same * value + other * partner(value)
        att[tick, pair_rows(my_pair), :] = (summed / mass).astype(BF16)

    def pair_rows(pair):
        return pl.ds(pl.multiple_of(pair * 128, 128), 128)

    def send_attended(tick):
        piece = att.at[tick, pair_rows(my_pair)]

        def send(i, _):
            far = (NZ - i + 1) // 2
            dev = on_line((z + NZ + far * (2 * (i % 2) - 1)) % NZ, core)
            push(piece, piece, at_send.at[tick], at_own.at[tick, my_pair // 2], s, dev)
            return 0

        lax.fori_loop(1, NZ, send, 0)

    def gather_attended(tick):
        for j in range(3):
            pair = j * 2 + core
            piece = att.at[tick, pair_rows(pair)]

            @pl.when(owner_of(pair, xl) != p)
            def _():
                take(piece, at_own.at[tick, j])

            push(piece, piece, at_send.at[tick], at_core.at[tick], s, core_mate)
        take(att.at[tick, pl.ds(0, 3 * 128)], at_core.at[tick])

    def project(tick, residual):
        out = jnp.where(
            first_half[: 2 * BLK], dot_nn(weven[...], att[tick]), dot_nn(wodd[...], att[tick])
        )
        out = out + pltpu.roll(out, 64, 1)
        out = jnp.where(first_half[:BLK], out[:BLK], out[BLK:])
        return (residual + gatev[tick] * out).astype(BF16)

    @pl.when(owned == 1)
    def _():
        attend(0)

    @pl.when(owned == 1)
    def _():
        send_attended(0)

    picked = [dot_nt(pick[j], xr[...]) for j in range(2)]
    residual = jnp.where(first_half[:BLK], picked[0], picked[1])
    take(wo.at[1 - xl], w_recv.at[2])
    for j in range(2):
        for pair in range(PAIRS):
            at = pl.ds(j * BLK, BLK), pl.ds(pair * 128, 128)
            weven[at] = wo[j, :, pl.ds(pair * 256, 128)]
            wodd[at] = wo[j, :, pl.ds(pair * 256 + 128, 128)]
    pf = lax.broadcasted_iota(jnp.int32, (CHUNK, 128), 0)
    po = lax.broadcasted_iota(jnp.int32, (CHUNK, 128), 1)
    for k in range(CHUNK // 128):
        to = po + (k % 3) * 128
        group = jnp.where(to >= 96, 1, 0) + jnp.where(to >= 192, 1, 0) + jnp.where(to >= 288, 1, 0)
        source = to + 96 * group + 96 * (k // 3)
        perm[:, pl.ds(k * 128, 128)] = jnp.where(pf == source, 1.0, 0.0).astype(BF16)
    half = CHUNK // 2
    for j in range(2):
        fold(1, j)
        for k in range(D // CHUNK):
            moved = dot_nn(wmod[1, j, :, pl.ds(k * CHUNK, CHUNK)], perm[...]).astype(BF16)
            wlow[j, :, pl.ds(k * half, half)] = moved[:, :half]
            whigh[j, :, pl.ds(k * half, half)] = moved[:, half:]

    gather_attended(0)
    ysrc[...] = project(0, residual)

    pl.semaphore_wait(nready, 1)
    spread(ysrc, g1.at[own], 1, after, 0)

    relay(g1, 1, 0)
    accs = []
    for j in range(2):
        acc = jnp.where(
            first_half[:QROWS], dot_nn(wlow[j], g1[...]), dot_nn(whigh[j], g1[...])
        )
        accs.append(acc + pltpu.roll(acc, 64, 1))
    total = jnp.zeros((128, 128), F32)
    for k in range(12):
        total += g1[pl.ds(k * 128, 128), :].astype(F32)
    total = jnp.sum(total, axis=0, keepdims=True)
    mean = (total + pltpu.roll(total, 64, 1)) * (1.0 / D)
    total = jnp.zeros((128, 128), F32)
    for k in range(12):
        centred = g1[pl.ds(k * 128, 128), :].astype(F32) - mean
        total += centred * centred
    total = jnp.sum(total, axis=0, keepdims=True)
    var = (total + pltpu.roll(total, 64, 1)) * (1.0 / D)
    for j in range(2):
        send_qkv(1, j, accs[j], mean, var)

    @pl.when(owned == 1)
    def _():
        unpack_stale(1)
        attend(1)

    @pl.when(owned == 1)
    def _():
        send_attended(1)

    gather_attended(1)
    last = project(1, g1[own, :].astype(F32)).astype(F32)
    blank = jnp.zeros((16, 128), F32)
    turned = jnp.transpose(
        jnp.concatenate([last, blank, pltpu.roll(last, 64, 1), blank], axis=0)
    )
    for i in range(LINE):
        for t in range(2):
            dsrc[i, pl.ds(t, 1), :] = turned[t * LINE + i : t * LINE + i + 1, :]

    def last_send(i, _):
        to = (me + i) % LINE
        push(dsrc.at[to], drecv.at[me], d_send, d_recv, after, on_line(to // 2, to % 2))
        return 0

    lax.fori_loop(0, LINE, last_send, 0)
    take(drecv, d_recv)
    out_ref[...] = drecv[...]
    finish(8)


def per_device(states, w_qkv, w_out, mod_table, q_gain, k_gain, stale_kv, timestep, patch_order):
    hbm = pl.BlockSpec(memory_space=pl.ANY)
    vmem = pl.BlockSpec(memory_space=pltpu.VMEM)
    dma = pltpu.SemaphoreType.DMA
    regular = pltpu.SemaphoreType.REGULAR
    got = pl.pallas_call(
        kernel,
        out_shape=jax.ShapeDtypeStruct((LINE, 2, 128), F32),
        in_specs=[hbm] * 5 + [vmem] * 3 + [pl.BlockSpec(memory_space=pltpu.SMEM)],
        out_specs=vmem,
        scratch_shapes=[
            pltpu.VMEM((2, D), BF16),
            pltpu.VMEM((2, QROWS, D), BF16),
            pltpu.VMEM((2, BLK, D // 2), BF16),
            pltpu.VMEM((84, 1, D), F32),
            pltpu.VMEM((2, 2, D), BF16),
            pltpu.VMEM((BLK, 128), F32),
            pltpu.VMEM((2, 96, 128), BF16),
            pltpu.VMEM((96, 128), BF16),
            pltpu.VMEM((96, 128), BF16),
            pltpu.VMEM((96, 128), F32),
            pltpu.VMEM((LINE * BLK, 128), BF16),
            pltpu.VMEM((LINE * BLK, 128), BF16),
            pltpu.VMEM((LINE * BLK, 128), F32),
            pltpu.VMEM((128, D), BF16),
            pltpu.VMEM((2, 2, QROWS, D), BF16),
            pltpu.VMEM((2 * BLK, D // 4), BF16),
            pltpu.VMEM((2 * BLK, D // 4), BF16),
            pltpu.VMEM((CHUNK, CHUNK), BF16),
            pltpu.VMEM((2, QROWS, D // 2), BF16),
            pltpu.VMEM((2, QROWS, D // 2), BF16),
            pltpu.VMEM((2, BLK, D), BF16),
            pltpu.VMEM((2, 2, 2, QROWS, 128), F32),
            pltpu.VMEM((2, BLK, 128), F32),
            pltpu.VMEM((2, 64, 128), F32),
            pltpu.VMEM((2, 128, 128), F32),
            pltpu.VMEM((2, 2, 9, 4, 128), F32),
            pltpu.VMEM((2, 2, 48, 4, 128), F32),
            pltpu.VMEM((3, 128, 128), F32),
            pltpu.VMEM((2, 512, 128), BF16),
            pltpu.VMEM((512, 128), F32),
            pltpu.VMEM((2, 2, 128, 128), BF16),
            pltpu.VMEM((2, 2, 128, 128), BF16),
            pltpu.VMEM((2, PAIRS * 128, 128), BF16),
            pltpu.VMEM((BLK, 128), BF16),
            pltpu.VMEM((LINE, 2, 128), F32),
            pltpu.VMEM((LINE, 2, 128), F32),
            dma((6,)),
            regular,
            dma((3,)),
            dma((3,)),
            dma((2,)),
            dma((2, NZ)),
            dma((2,)),
            dma((2,)),
            dma((2,)),
            dma((2,)),
            dma((2,)),
            dma((2,)),
            dma((2, 3)),
            dma((2,)),
            dma,
            dma,
        ],
        compiler_params=pltpu.CompilerParams(
            collective_id=0, has_side_effects=True, vmem_limit_bytes=56 * 2**20
        ),
        name="block_cycle",
    )(
        states[0],
        w_qkv[0].T,
        w_out[0].T,
        jnp.transpose(mod_table, (0, 2, 1, 3)).reshape(84, 1, D),
        stale_kv[0],
        patch_order.reshape(1, 64),
        q_gain,
        k_gain,
        timestep,
    )
    split = got.reshape(NZ, 2, 2, 2, 64)[..., :BLK]
    return jnp.transpose(split, (2, 0, 3, 1, 4)).reshape(1, 2, D).astype(BF16)


def solution(mesh):
    in_specs = (
        P("section", "patch", None),
        P("section", None, "patch"),
        P("section", None, "patch"),
        P(None, "section", None, None),
        P("section", None),
        P("section", None),
        P("section", None, "patch", None),
        P(),
        P(),
    )
    out_specs = P("section", "patch", None)
    return jax.shard_map(
        per_device, mesh=mesh, in_specs=in_specs, out_specs=out_specs, check_vma=False
    )
```

```python
import jax
import jax.numpy as jnp
from jax import lax
from jax.experimental import pallas as pl
from jax.experimental.pallas import tpu as pltpu
from jax.sharding import PartitionSpec as P

MESH = pl.DeviceIdType.MESH
F32 = jnp.float32
BF16 = jnp.bfloat16
NZ = 16
NS = 8
BLK = 48
HEADS = 12
PAIRS = 6
D = 3072
KC = D // 128
LINE = 32
QROWS = 72
REACH = 4
CHUNK = 768


def owner_of(pair, line):
    part = ((pair + line) % 3) * PAIRS + pair
    centre = (32 * part + 16) // 9
    return (centre // 4) * 4 + 2 * line + pair % 2


def dot_nt(a, b):
    return lax.dot_general(a, b, (((1,), (1,)), ((), ())), preferred_element_type=F32)


def dot_nn(a, b):
    return lax.dot_general(a, b, (((1,), (0,)), ((), ())), preferred_element_type=F32)


def kernel(
    x_hbm, wq_hbm, wo_hbm, mod_hbm, st_hbm, order_ref, qg_ref, kg_ref, time_ref,
    out_ref,
    x_in, wq, wo, mod, st_in, rows_f, st_src, st_own, st_mate, gran_f,
    g0, g1, wide, xr, wmod, wodd, weven, perm, wline, pick, colv, gatev, table, gains,
    qsrc, qrecv, merged, stale, stale_f, keys, vals, att, ysrc, dsrc, drecv,
    load_sem, nready, w_send, w_recv,
    ag_send, ag_own, ag_core,
    st_send, st_recv, q_send, q_recv,
    at_send, at_own, at_core,
    d_send, d_recv,
):
    s = lax.axis_index("section")
    p = lax.axis_index("patch")
    z = p // 4
    xl = (p // 2) % 2
    core = p % 2
    me = z * 2 + core
    after = (s + 1) % NS
    before = (s + NS - 1) % NS
    core_mate = z * 4 + xl * 2 + (1 - core)
    x_mate = z * 4 + (1 - xl) * 2 + core

    def on_line(zs, c):
        return zs * 4 + xl * 2 + c

    loads = [
        pltpu.make_async_copy(x_hbm, x_in, load_sem.at[0]),
        pltpu.make_async_copy(st_hbm.at[s], st_in.at[0], load_sem.at[1]),
        pltpu.make_async_copy(st_hbm.at[before], st_in.at[1], load_sem.at[2]),
        pltpu.make_async_copy(wq_hbm, wq.at[xl], load_sem.at[3]),
        pltpu.make_async_copy(wo_hbm, wo.at[xl], load_sem.at[4]),
        pltpu.make_async_copy(mod_hbm, mod, load_sem.at[5]),
    ]
    for load in loads:
        load.start()

    barrier = pltpu.get_barrier_semaphore()

    def greet(sec, dev):
        pl.semaphore_signal(barrier, inc=1, device_id=(sec, dev), device_id_type=MESH)

    for far in range(1, REACH + 1):
        greet(s, on_line((z + far) % NZ, core))
        greet(s, on_line((z + NZ - far) % NZ, core))
    greet(s, core_mate)
    greet(s, x_mate)
    greet(after, p)
    greet(before, p)

    loads[0].wait()
    xf = x_in[...].astype(F32)
    for t in range(2):
        for k in range(KC):
            rows_f[pl.ds(t * KC + k, 1), :] = xf[t : t + 1, k * 128 : (k + 1) * 128]
    own = pl.ds(pl.multiple_of(me * BLK, 16), BLK)
    g0[own, :] = rows_f[...].astype(BF16)
    def block(g, b):
        return g.at[pl.ds(pl.multiple_of(b * BLK, 16), BLK)]

    def push(src, dst, send, recv, sec, dev):
        pltpu.make_async_remote_copy(
            src_ref=src, dst_ref=dst, send_sem=send, recv_sem=recv,
            device_id=(sec, dev), device_id_type=MESH,
        ).start()

    def take(ref, sem):
        pltpu.make_async_copy(ref, ref, sem).wait()

    routes = []
    for j in range(2):
        for i in range(9):
            unit = (z * 4 + 2 * j + core) * 9 + i
            part = unit // 16
            head = part % HEADS
            dev = owner_of(head // 2, xl)
            routes.append((dev, head % 2, (part // HEADS) * 16 + unit % 16))

    my_pair = jnp.int32(0)
    owned = jnp.int32(0)
    for pair in range(PAIRS):
        hit = jnp.where(p == owner_of(pair, xl), 1, 0)
        my_pair = my_pair + pair * hit
        owned = owned + hit

    def drain_stale(tick):
        def step(i, _):
            take(st_src.at[tick, pl.ds(0, 16)], st_send.at[tick])
            return 0

        lax.fori_loop(0, PAIRS - owned, step, 0)

    def finish(stage):
        if stage == 1:
            for load in loads[4:]:
                load.wait()
        if stage == 2:
            @pl.when(owned == 1)
            def _():
                take(stale.at[0], st_recv.at[0])
            take(wq.at[1 - xl], w_recv.at[0])
        if 3 <= stage < 6:
            @pl.when(owned == 1)
            def _():
                take(stale.at[1], st_recv.at[1])
        if 2 <= stage < 5:
            pl.semaphore_wait(nready, 1)
        if stage >= 2:
            take(g0.at[pl.ds(0, 31 * BLK)], ag_send.at[0])
            take(wq.at[xl], w_send.at[0])
            take(wo.at[xl], w_send.at[2])

            drain_stale(0)
            take(st_own, w_send.at[1])
        if 2 <= stage < 4:
            take(wo.at[1 - xl], w_recv.at[2])
        if stage >= 3:
            drain_stale(1)
        if stage >= 5:
            take(g1, ag_send.at[1])
        if stage >= 8:
            take(dsrc, d_send)
        mine_units = jnp.int32(0)
        for dev, _, _ in routes:
            mine_units = mine_units + jnp.where(dev == p, 1, 0)
        for tick in range(2):
            def drain(i, _):
                take(qsrc.at[tick, 0, 0], q_send.at[tick])
                return 0

            if stage >= 3 + 3 * tick:
                lax.fori_loop(0, 18 - mine_units, drain, 0)
            if stage >= 4 + 3 * tick:
                def drain_piece(i, _):
                    take(att.at[tick, pl.ds(0, 128)], at_send.at[tick])
                    return 0

                lax.fori_loop(0, 3 + (NZ - 1) * owned, drain_piece, 0)

    def relay_core(g, tick, zs):
        b = zs * 2 + core
        push(block(g, b), block(g, b), ag_send.at[tick], ag_core.at[tick], s, core_mate)

    def arrive(g, tick, i):
        far = (i + 1) // 2
        zs = (z + NZ - far * (2 * (i % 2) - 1)) % NZ
        take(block(g, zs * 2 + core), ag_own.at[tick, zs])
        return zs

    def near_step(g, tick):
        def step(i, _):
            relay_core(g, tick, arrive(g, tick, i))
            return 0

        return step

    def relay(g, tick, first, between=None):
        edge = []
        for i in (2 * REACH - 1, 2 * REACH):
            zs = arrive(g, tick, i)
            edge.append(zs)
            sign = 2 * (i % 2) - 1
            piece = block(g, zs * 2 + core)
            for far in range(REACH - 1 + i % 2, 0, -1):
                dev = on_line((z + NZ + sign * far) % NZ, core)
                push(piece, piece, ag_send.at[tick], ag_own.at[tick, zs], s, dev)
        lax.fori_loop(first, 2 * REACH - 1, near_step(g, tick), 0)
        for zs in edge:
            relay_core(g, tick, zs)
        if between is not None:
            between()
        lax.fori_loop(2 * REACH + 1, NZ, near_step(g, tick), 0)
        take(g.at[pl.ds(0, NZ * BLK)], ag_core.at[tick])

    def spread(src, dst, tick, sec, first):
        def send(far, sign):
            dev = on_line((z + NZ + sign * far) % NZ, core)
            push(src, dst, ag_send.at[tick], ag_own.at[tick, z], sec, dev)

        send(REACH, 1)
        send(REACH, -1)
        for far in range(REACH - 1, 0, -1):
            send(far, 1)
            send(far, -1)
        if first == 0:
            send(0, 1)

    loads[1].wait()
    loads[2].wait()
    for tick in range(2):
        sf = st_in[tick].astype(F32)
        for kv in range(2):
            for head in range(HEADS):
                for t in range(2):
                    row = tick * 48 + (head // 2) * 8 + ((head % 2) * 2 + kv) * 2 + t
                    low = (kv * HEADS + head) * 128
                    gran_f[pl.ds(row, 1), :] = sf[t : t + 1, low : low + 128]
    st_own[...] = gran_f[...].astype(BF16)
    loads[3].wait()

    pl.semaphore_wait(barrier, 2 * REACH + 4)

    spread(g0.at[own], g0.at[own], 0, s, 1)
    relay_core(g0, 0, z)
    push(st_own, st_mate, w_send.at[1], w_recv.at[1], s, x_mate)
    push(wq.at[xl], wq.at[xl], w_send.at[0], w_recv.at[0], s, x_mate)
    loads[4].wait()
    loads[5].wait()


    times = [time_ref[s], time_ref[before]]
    lane = lax.broadcasted_iota(jnp.int32, (128, 128), 1)
    first_half = lane < 64

    def fold(tick, j):
        shift_sum = jnp.zeros((QROWS, 128), F32)
        row_sum = jnp.zeros((QROWS, 128), F32)
        base = times[tick] * 3
        for k in range(KC):
            lanes = pl.ds(k * 128, 128)
            shift = mod[base, :, lanes]
            scale = mod[base + 1, :, lanes]
            w = wq[j, :, lanes].astype(F32)
            scaled = (w * (1.0 + scale)).astype(BF16)
            wmod[tick, j, :, lanes] = scaled
            shift_sum += w * shift
            row_sum += scaled.astype(F32)
        for n, value in enumerate((shift_sum, row_sum)):
            total = jnp.sum(value, axis=1, keepdims=True)
            colv[tick, n, j] = jnp.broadcast_to(total, (QROWS, 128))

    fold(0, xl)

    feature = lax.broadcasted_iota(jnp.int32, (BLK, 128), 1)
    row = lax.broadcasted_iota(jnp.int32, (BLK, 128), 0)
    gate_sums = []
    for j in range(2):
        mine = (z * 4 + 2 * j + core) * BLK + row
        sums = [jnp.zeros((BLK, 128), F32), jnp.zeros((BLK, 128), F32)]
        for k in range(KC):
            lanes = pl.ds(k * 128, 128)
            here = feature + k * 128 == mine
            pick[j, :, lanes] = jnp.where(here, 1.0, 0.0).astype(BF16)
            for tick in range(2):
                sums[tick] += jnp.where(here, mod[times[tick] * 3 + 2, :, lanes], 0.0)
        gate_sums.append([jnp.sum(v, axis=1, keepdims=True) for v in sums])
    for tick in range(2):
        gatev[tick] = jnp.where(first_half[:BLK], gate_sums[0][tick], gate_sums[1][tick])

    @pl.when(owned == 1)
    def _():
        r = lax.broadcasted_iota(jnp.int32, (128, 128), 0)
        for j, ref in enumerate((qg_ref, kg_ref)):
            diag = jnp.where(r == lane, jnp.broadcast_to(ref[...], (128, 128)), 0.0)
            gains[j] = jnp.broadcast_to(jnp.sum(diag, axis=1, keepdims=True), (128, 128))
        pr = r[:64]
        pc = lane[:64]
        places = jnp.broadcast_to(order_ref[...].astype(F32), (64, 64))
        column = jnp.sum(
            jnp.where(pr[:, :64] == pc[:, :64], places, 0.0), axis=1, keepdims=True
        )
        token = pc % 64
        patch = ((token % LINE) // 2) * 4 + 2 * xl + token % 2
        place = jnp.sum(jnp.where(pr == patch, column, 0.0), axis=0, keepdims=True)
        pos = place * 2.0 + jnp.where(token[:1] < LINE, 0.0, 1.0)
        freq = jnp.exp(pr.astype(F32) * (-jnp.log(F32(10000.0)) / 64.0))
        angle = pos * freq
        table[0] = jnp.cos(angle)
        table[1] = jnp.sin(angle)

    def build_stale():
        take(st_mate, w_recv.at[1])
        other_f = st_mate[...].astype(F32)
        own_f = gran_f[...]
        low_f = jnp.where(xl == 0, own_f, other_f)
        high_f = jnp.where(xl == 0, other_f, own_f)
        for tick in range(2):
            for pair in range(PAIRS):
                low = tick * 48 + pair * 8
                both = jnp.concatenate([low_f[low : low + 8], high_f[low : low + 8]], axis=0)
                st_src[tick, pl.ds(pair * 16, 16), :] = both.astype(BF16)

    relay(g0, 0, 1, build_stale)
    pl.semaphore_signal(nready, inc=1, device_id=(before, p), device_id_type=MESH)

    def send_stale(tick):
        for pair in range(PAIRS):
            dev = owner_of(pair, xl)
            src = st_src.at[tick, pl.ds(pair * 16, 16)]
            dst = stale.at[tick, pl.ds(pl.multiple_of(me * 16, 16), 16)]

            @pl.when(p == dev)
            def _():
                pltpu.make_async_copy(src, dst, st_recv.at[tick]).start()

            @pl.when(p != dev)
            def _():
                push(src, dst, st_send.at[tick], st_recv.at[tick], s, dev)

    send_stale(0)


    def send_qkv(tick, j, acc, mean, var):
        static = isinstance(j, int)
        qkv = lax.rsqrt(var + 1e-06) * (acc - colv[tick, 1, j] * mean) + colv[tick, 0, j]
        qkv = qkv.astype(BF16).astype(F32)
        for i in range(9):
            top, bottom = qkv[i * 8 : i * 8 + 4], qkv[i * 8 + 4 : i * 8 + 8]
            qsrc[tick, j, i] = jnp.where(first_half[:4], top, bottom)
        for i in range(9):
            if static:
                dev, half, slot = routes[j * 9 + i]
            else:
                dev, half, slot = [
                    jnp.where(j == 0, a, b) for a, b in zip(routes[i], routes[9 + i])
                ]
            src = qsrc.at[tick, j, i]
            dst = qrecv.at[tick, half, slot]

            @pl.when(p == dev)
            def _():
                pltpu.make_async_copy(src, dst, q_recv.at[tick]).start()

            @pl.when(p != dev)
            def _():
                push(src, dst, q_send.at[tick], q_recv.at[tick], s, dev)

    for b in range(12):
        part = pl.ds(b * 128, 128)
        wide[part, :] = g0[part, :].astype(F32)
    total = jnp.zeros((64, 128), F32)
    for k in range(KC):
        lanes = pl.ds(k * 128, 128)
        piece = jnp.concatenate(
            [wide[pl.ds(t * KC + k, LINE, stride=BLK), :] for t in range(2)], axis=0
        )
        total += piece
        narrow = piece.astype(BF16)
        xr[pl.ds(0, 64), lanes] = narrow
        xr[pl.ds(64, 64), lanes] = narrow
    acc_own = dot_nt(wmod[0, xl], xr[...])
    mean_c = jnp.sum(total, axis=1, keepdims=True) * (1.0 / D)
    total = jnp.zeros((64, 128), F32)
    for k in range(KC):
        centred = xr[pl.ds(0, 64), pl.ds(k * 128, 128)].astype(F32) - mean_c
        total += centred * centred
    var_c = jnp.sum(total, axis=1, keepdims=True) * (1.0 / D)
    stats = jnp.where(first_half[:64], mean_c, var_c)
    stats = jnp.transpose(jnp.concatenate([stats, stats], axis=0))
    mean0, var0 = stats[0:1, :], stats[64:65, :]
    send_qkv(0, xl, acc_own, mean0, var0)
    take(wq.at[1 - xl], w_recv.at[0])
    push(wo.at[xl], wo.at[xl], w_send.at[2], w_recv.at[2], s, x_mate)
    fold(0, 1 - xl)
    send_qkv(0, 1 - xl, dot_nt(wmod[0, 1 - xl], xr[...]), mean0, var0)
    send_stale(1)

    def unpack_stale(tick):
        take(stale.at[tick], st_recv.at[tick])
        for b in range(4):
            part = pl.ds(b * 128, 128)
            stale_f[part, :] = stale[tick, part, :].astype(F32)
        for second in range(2):
            got = []
            for kv in range(2):
                pieces = [
                    stale_f[pl.ds(line * 8 + (second * 2 + kv) * 2 + t, LINE, stride=16), :]
                    for t in range(2)
                    for line in range(2)
                ]
                got.append(jnp.concatenate(pieces, axis=0))
            keys[tick, second] = got[0].astype(BF16)
            vals[tick, second] = jnp.transpose(got[1]).astype(BF16)

    @pl.when(owned == 1)
    def _():
        unpack_stale(0)

    def attend(tick):
        take(qrecv.at[tick], q_recv.at[tick])
        factor = 128.0 ** -0.5
        cosine, sine = table[0], table[1]

        def received(kind):
            left = first_half[:4]
            for i in range(16):
                first, second = qrecv[tick, 0, kind * 16 + i], qrecv[tick, 1, kind * 16 + i]
                merged[kind, pl.ds(i * 8, 4), :] = jnp.where(
                    left, first, pltpu.roll(second, 64, 1)
                )
                merged[kind, pl.ds(i * 8 + 4, 4), :] = jnp.where(
                    left, pltpu.roll(first, 64, 1), second
                )
            return merged[kind]

        def prepared(j):
            u = received(j)
            square = jnp.sum(u * u, axis=0, keepdims=True) * (1.0 / 128)
            u = u * lax.rsqrt(square + 1e-06) * gains[j]
            a, b = u[:64], u[64:]
            return jnp.concatenate(
                [a * cosine - b * sine, a * sine + b * cosine], axis=0
            ).astype(BF16)

        def partner(u):
            up = pltpu.roll(u, 128 - LINE, 1)
            down = pltpu.roll(u, LINE, 1)
            return jnp.where(lane % 64 < LINE, up, down)

        query = prepared(0)
        key = prepared(1).astype(F32)
        value = received(2)
        scores = jnp.where(
            first_half, dot_nn(keys[tick, 0], query), dot_nn(keys[tick, 1], query)
        ) * factor
        r = lax.broadcasted_iota(jnp.int32, (128, 128), 0)
        key_line = (r // LINE) % 2
        own_patch = (r % LINE == lane % LINE) & (key_line == xl)
        scores = jnp.where(own_patch, -1e30, scores)
        wide_q = query.astype(F32)
        same = jnp.sum(wide_q * key, axis=0, keepdims=True) * factor
        other = jnp.sum(wide_q * partner(key), axis=0, keepdims=True) * factor
        top = jnp.maximum(jnp.max(scores, axis=0, keepdims=True), jnp.maximum(same, other))
        weights = jnp.exp(scores - top)
        same = jnp.exp(same - top)
        other = jnp.exp(other - top)
        mass = jnp.sum(weights, axis=0, keepdims=True) + same + other
        weights = weights.astype(BF16)
        summed = jnp.where(
            first_half, dot_nn(vals[tick, 0], weights), dot_nn(vals[tick, 1], weights)
        )
        summed = summed + same * value + other * partner(value)
        att[tick, pair_rows(my_pair), :] = (summed / mass).astype(BF16)

    def pair_rows(pair):
        return pl.ds(pl.multiple_of(pair * 128, 128), 128)

    def send_attended(tick):
        piece = att.at[tick, pair_rows(my_pair)]

        def send(i, _):
            far = (NZ - i + 1) // 2
            dev = on_line((z + NZ + far * (2 * (i % 2) - 1)) % NZ, core)
            push(piece, piece, at_send.at[tick], at_own.at[tick, my_pair // 2], s, dev)
            return 0

        lax.fori_loop(1, NZ, send, 0)

    def gather_attended(tick):
        for j in range(3):
            pair = j * 2 + core
            piece = att.at[tick, pair_rows(pair)]

            @pl.when(owner_of(pair, xl) != p)
            def _():
                take(piece, at_own.at[tick, j])

            push(piece, piece, at_send.at[tick], at_core.at[tick], s, core_mate)
        take(att.at[tick, pl.ds(0, 3 * 128)], at_core.at[tick])

    def project(tick, residual):
        out = jnp.where(
            first_half[: 2 * BLK], dot_nn(weven[...], att[tick]), dot_nn(wodd[...], att[tick])
        )
        out = out + pltpu.roll(out, 64, 1)
        out = jnp.where(first_half[:BLK], out[:BLK], out[BLK:])
        return (residual + gatev[tick] * out).astype(BF16)

    @pl.when(owned == 1)
    def _():
        attend(0)

    @pl.when(owned == 1)
    def _():
        send_attended(0)

    picked = [dot_nt(pick[j], xr[...]) for j in range(2)]
    residual = jnp.where(first_half[:BLK], picked[0], picked[1])
    take(wo.at[1 - xl], w_recv.at[2])
    for j in range(2):
        for pair in range(PAIRS):
            at = pl.ds(j * BLK, BLK), pl.ds(pair * 128, 128)
            weven[at] = wo[j, :, pl.ds(pair * 256, 128)]
            wodd[at] = wo[j, :, pl.ds(pair * 256 + 128, 128)]
    pf = lax.broadcasted_iota(jnp.int32, (CHUNK, 128), 0)
    po = lax.broadcasted_iota(jnp.int32, (CHUNK, 128), 1)
    for k in range(CHUNK // 128):
        to = po + (k % 3) * 128
        group = jnp.where(to >= 96, 1, 0) + jnp.where(to >= 192, 1, 0) + jnp.where(to >= 288, 1, 0)
        source = to + 96 * group + 96 * (k // 3)
        perm[:, pl.ds(k * 128, 128)] = jnp.where(pf == source, 1.0, 0.0).astype(BF16)
    half = CHUNK // 2
    for j in range(2):
        fold(1, j)
        for k in range(D // CHUNK):
            moved = dot_nn(wmod[1, j, :, pl.ds(k * CHUNK, CHUNK)], perm[...])
            moved = jnp.concatenate([moved, jnp.zeros((8, CHUNK), F32)], axis=0).astype(BF16)
            lanes = pl.ds(k * half, half)
            wline[pl.ds(j * 160, 80), lanes] = moved[:, :half]
            wline[pl.ds(j * 160 + 80, 80), lanes] = moved[:, half:]

    gather_attended(0)
    ysrc[...] = project(0, residual)

    pl.semaphore_wait(nready, 1)
    spread(ysrc, g1.at[own], 1, after, 0)

    relay(g1, 1, 0)
    product = dot_nn(wline[...], g1[...])
    accs = []
    for j in range(2):
        low, high = product[j * 160 : j * 160 + QROWS], product[j * 160 + 80 : j * 160 + 80 + QROWS]
        acc = jnp.where(first_half[:QROWS], low, high)
        accs.append(acc + pltpu.roll(acc, 64, 1))
    total = jnp.zeros((128, 128), F32)
    for k in range(12):
        total += g1[pl.ds(k * 128, 128), :].astype(F32)
    total = jnp.sum(total, axis=0, keepdims=True)
    mean = (total + pltpu.roll(total, 64, 1)) * (1.0 / D)
    total = jnp.zeros((128, 128), F32)
    for k in range(12):
        centred = g1[pl.ds(k * 128, 128), :].astype(F32) - mean
        total += centred * centred
    total = jnp.sum(total, axis=0, keepdims=True)
    var = (total + pltpu.roll(total, 64, 1)) * (1.0 / D)
    for j in range(2):
        send_qkv(1, j, accs[j], mean, var)

    @pl.when(owned == 1)
    def _():
        unpack_stale(1)
        attend(1)

    @pl.when(owned == 1)
    def _():
        send_attended(1)

    gather_attended(1)
    last = project(1, g1[own, :].astype(F32)).astype(F32)
    blank = jnp.zeros((16, 128), F32)
    turned = jnp.transpose(
        jnp.concatenate([last, blank, pltpu.roll(last, 64, 1), blank], axis=0)
    )
    for i in range(LINE):
        for t in range(2):
            dsrc[i, pl.ds(t, 1), :] = turned[t * LINE + i : t * LINE + i + 1, :]

    def last_send(i, _):
        to = (me + LINE // 2 + LINE + (i + 1) // 2 * (2 * (i % 2) - 1)) % LINE
        push(dsrc.at[to], drecv.at[me], d_send, d_recv, after, on_line(to // 2, to % 2))
        return 0

    lax.fori_loop(0, LINE, last_send, 0)
    take(drecv, d_recv)
    out_ref[...] = drecv[...]
    finish(8)


def per_device(states, w_qkv, w_out, mod_table, q_gain, k_gain, stale_kv, timestep, patch_order):
    hbm = pl.BlockSpec(memory_space=pl.ANY)
    vmem = pl.BlockSpec(memory_space=pltpu.VMEM)
    dma = pltpu.SemaphoreType.DMA
    regular = pltpu.SemaphoreType.REGULAR
    got = pl.pallas_call(
        kernel,
        out_shape=jax.ShapeDtypeStruct((LINE, 2, 128), F32),
        in_specs=[hbm] * 5 + [vmem] * 3 + [pl.BlockSpec(memory_space=pltpu.SMEM)],
        out_specs=vmem,
        scratch_shapes=[
            pltpu.VMEM((2, D), BF16),
            pltpu.VMEM((2, QROWS, D), BF16),
            pltpu.VMEM((2, BLK, D // 2), BF16),
            pltpu.VMEM((84, 1, D), F32),
            pltpu.VMEM((2, 2, D), BF16),
            pltpu.VMEM((BLK, 128), F32),
            pltpu.VMEM((2, 96, 128), BF16),
            pltpu.VMEM((96, 128), BF16),
            pltpu.VMEM((96, 128), BF16),
            pltpu.VMEM((96, 128), F32),
            pltpu.VMEM((LINE * BLK, 128), BF16),
            pltpu.VMEM((LINE * BLK, 128), BF16),
            pltpu.VMEM((LINE * BLK, 128), F32),
            pltpu.VMEM((128, D), BF16),
            pltpu.VMEM((2, 2, QROWS, D), BF16),
            pltpu.VMEM((2 * BLK, D // 4), BF16),
            pltpu.VMEM((2 * BLK, D // 4), BF16),
            pltpu.VMEM((CHUNK, CHUNK), BF16),
            pltpu.VMEM((320, D // 2), BF16),
            pltpu.VMEM((2, BLK, D), BF16),
            pltpu.VMEM((2, 2, 2, QROWS, 128), F32),
            pltpu.VMEM((2, BLK, 128), F32),
            pltpu.VMEM((2, 64, 128), F32),
            pltpu.VMEM((2, 128, 128), F32),
            pltpu.VMEM((2, 2, 9, 4, 128), F32),
            pltpu.VMEM((2, 2, 48, 4, 128), F32),
            pltpu.VMEM((3, 128, 128), F32),
            pltpu.VMEM((2, 512, 128), BF16),
            pltpu.VMEM((512, 128), F32),
            pltpu.VMEM((2, 2, 128, 128), BF16),
            pltpu.VMEM((2, 2, 128, 128), BF16),
            pltpu.VMEM((2, PAIRS * 128, 128), BF16),
            pltpu.VMEM((BLK, 128), BF16),
            pltpu.VMEM((LINE, 2, 128), F32),
            pltpu.VMEM((LINE, 2, 128), F32),
            dma((6,)),
            regular,
            dma((3,)),
            dma((3,)),
            dma((2,)),
            dma((2, NZ)),
            dma((2,)),
            dma((2,)),
            dma((2,)),
            dma((2,)),
            dma((2,)),
            dma((2,)),
            dma((2, 3)),
            dma((2,)),
            dma,
            dma,
        ],
        compiler_params=pltpu.CompilerParams(
            collective_id=0, has_side_effects=True, vmem_limit_bytes=56 * 2**20
        ),
        name="block_cycle",
    )(
        states[0],
        w_qkv[0].T,
        w_out[0].T,
        jnp.transpose(mod_table, (0, 2, 1, 3)).reshape(84, 1, D),
        stale_kv[0],
        patch_order.reshape(1, 64),
        q_gain,
        k_gain,
        timestep,
    )
    split = got.reshape(NZ, 2, 2, 2, 64)[..., :BLK]
    return jnp.transpose(split, (2, 0, 3, 1, 4)).reshape(1, 2, D).astype(BF16)


def solution(mesh):
    in_specs = (
        P("section", "patch", None),
        P("section", None, "patch"),
        P("section", None, "patch"),
        P(None, "section", None, None),
        P("section", None),
        P("section", None),
        P("section", None, "patch", None),
        P(),
        P(),
    )
    out_specs = P("section", "patch", None)
    return jax.shard_map(
        per_device, mesh=mesh, in_specs=in_specs, out_specs=out_specs, check_vma=False
    )
```

```python
import jax
import jax.numpy as jnp
from jax import lax
from jax.experimental import pallas as pl
from jax.experimental.pallas import tpu as pltpu
from jax.sharding import PartitionSpec as P

MESH = pl.DeviceIdType.MESH
F32 = jnp.float32
BF16 = jnp.bfloat16
NZ = 16
NS = 8
BLK = 48
HEADS = 12
PAIRS = 6
D = 3072
KC = D // 128
LINE = 32
QROWS = 72
REACH = 4
CHUNK = 768


def owner_of(pair, line):
    part = ((pair + line) % 3) * PAIRS + pair
    centre = (32 * part + 16) // 9
    return (centre // 4) * 4 + 2 * line + pair % 2


def dot_nt(a, b):
    return lax.dot_general(a, b, (((1,), (1,)), ((), ())), preferred_element_type=F32)


def dot_nn(a, b):
    return lax.dot_general(a, b, (((1,), (0,)), ((), ())), preferred_element_type=F32)


def kernel(
    x_hbm, wq_hbm, wo_hbm, mod_hbm, st_hbm, order_ref, qg_ref, kg_ref, time_ref,
    out_ref,
    x_in, wq, wo, mod, st_in, rows_f, st_src, st_own, st_mate, gran_f,
    g0, g1, wide, xr, wmod, wstack, wodd, weven, perm, wline, pick, colv, gatev, table, gains,
    qsrc, qrecv, merged, stale, stale_f, keys, vals, att, ysrc, dsrc, drecv,
    load_sem, nready, w_send, w_recv,
    ag_send, ag_own, ag_core,
    st_send, st_recv, q_send, q_recv,
    at_send, at_own, at_core,
    d_send, d_recv,
):
    s = lax.axis_index("section")
    p = lax.axis_index("patch")
    z = p // 4
    xl = (p // 2) % 2
    core = p % 2
    me = z * 2 + core
    after = (s + 1) % NS
    before = (s + NS - 1) % NS
    core_mate = z * 4 + xl * 2 + (1 - core)
    x_mate = z * 4 + (1 - xl) * 2 + core

    def on_line(zs, c):
        return zs * 4 + xl * 2 + c

    loads = [
        pltpu.make_async_copy(x_hbm, x_in, load_sem.at[0]),
        pltpu.make_async_copy(st_hbm.at[s], st_in.at[0], load_sem.at[1]),
        pltpu.make_async_copy(st_hbm.at[before], st_in.at[1], load_sem.at[2]),
        pltpu.make_async_copy(wq_hbm, wq.at[xl], load_sem.at[3]),
        pltpu.make_async_copy(wo_hbm, wo.at[xl], load_sem.at[4]),
        pltpu.make_async_copy(mod_hbm, mod, load_sem.at[5]),
    ]
    for load in loads:
        load.start()

    barrier = pltpu.get_barrier_semaphore()

    def greet(sec, dev):
        pl.semaphore_signal(barrier, inc=1, device_id=(sec, dev), device_id_type=MESH)

    for far in range(1, REACH + 1):
        greet(s, on_line((z + far) % NZ, core))
        greet(s, on_line((z + NZ - far) % NZ, core))
    greet(s, core_mate)
    greet(s, x_mate)
    greet(after, p)
    greet(before, p)

    loads[0].wait()
    xf = x_in[...].astype(F32)
    for t in range(2):
        for k in range(KC):
            rows_f[pl.ds(t * KC + k, 1), :] = xf[t : t + 1, k * 128 : (k + 1) * 128]
    own = pl.ds(pl.multiple_of(me * BLK, 16), BLK)
    g0[own, :] = rows_f[...].astype(BF16)
    def block(g, b):
        return g.at[pl.ds(pl.multiple_of(b * BLK, 16), BLK)]

    def push(src, dst, send, recv, sec, dev):
        pltpu.make_async_remote_copy(
            src_ref=src, dst_ref=dst, send_sem=send, recv_sem=recv,
            device_id=(sec, dev), device_id_type=MESH,
        ).start()

    def take(ref, sem):
        pltpu.make_async_copy(ref, ref, sem).wait()

    routes = []
    for j in range(2):
        for i in range(9):
            unit = (z * 4 + 2 * j + core) * 9 + i
            part = unit // 16
            head = part % HEADS
            dev = owner_of(head // 2, xl)
            routes.append((dev, head % 2, (part // HEADS) * 16 + unit % 16))

    my_pair = jnp.int32(0)
    owned = jnp.int32(0)
    for pair in range(PAIRS):
        hit = jnp.where(p == owner_of(pair, xl), 1, 0)
        my_pair = my_pair + pair * hit
        owned = owned + hit

    def drain_stale(tick):
        def step(i, _):
            take(st_src.at[tick, pl.ds(0, 16)], st_send.at[tick])
            return 0

        lax.fori_loop(0, PAIRS - owned, step, 0)

    def finish(stage):
        if stage == 1:
            for load in loads[4:]:
                load.wait()
        if stage == 2:
            @pl.when(owned == 1)
            def _():
                take(stale.at[0], st_recv.at[0])
            take(wq.at[1 - xl], w_recv.at[0])
        if 3 <= stage < 6:
            @pl.when(owned == 1)
            def _():
                take(stale.at[1], st_recv.at[1])
        if 2 <= stage < 5:
            pl.semaphore_wait(nready, 1)
        if stage >= 2:
            take(g0.at[pl.ds(0, 31 * BLK)], ag_send.at[0])
            take(wq.at[xl], w_send.at[0])
            take(wo.at[xl], w_send.at[2])

            drain_stale(0)
            take(st_own, w_send.at[1])
        if 2 <= stage < 4:
            take(wo.at[1 - xl], w_recv.at[2])
        if stage >= 3:
            drain_stale(1)
        if stage >= 5:
            take(g1, ag_send.at[1])
        if stage >= 8:
            take(dsrc, d_send)
        mine_units = jnp.int32(0)
        for dev, _, _ in routes:
            mine_units = mine_units + jnp.where(dev == p, 1, 0)
        for tick in range(2):
            def drain(i, _):
                take(qsrc.at[tick, 0, 0], q_send.at[tick])
                return 0

            if stage >= 3 + 3 * tick:
                lax.fori_loop(0, 18 - mine_units, drain, 0)
            if stage >= 4 + 3 * tick:
                def drain_piece(i, _):
                    take(att.at[tick, pl.ds(0, 128)], at_send.at[tick])
                    return 0

                lax.fori_loop(0, 3 + (NZ - 1) * owned, drain_piece, 0)

    def relay_core(g, tick, zs):
        b = zs * 2 + core
        push(block(g, b), block(g, b), ag_send.at[tick], ag_core.at[tick], s, core_mate)

    def arrive(g, tick, i):
        far = (i + 1) // 2
        zs = (z + NZ - far * (2 * (i % 2) - 1)) % NZ
        take(block(g, zs * 2 + core), ag_own.at[tick, zs])
        return zs

    def near_step(g, tick):
        def step(i, _):
            relay_core(g, tick, arrive(g, tick, i))
            return 0

        return step

    def relay(g, tick, first, between=None):
        edge = []
        for i in (2 * REACH - 1, 2 * REACH):
            zs = arrive(g, tick, i)
            edge.append(zs)
            sign = 2 * (i % 2) - 1
            piece = block(g, zs * 2 + core)
            for far in range(REACH - 1 + i % 2, 0, -1):
                dev = on_line((z + NZ + sign * far) % NZ, core)
                push(piece, piece, ag_send.at[tick], ag_own.at[tick, zs], s, dev)
        lax.fori_loop(first, 2 * REACH - 1, near_step(g, tick), 0)
        for zs in edge:
            relay_core(g, tick, zs)
        if between is not None:
            between()
        lax.fori_loop(2 * REACH + 1, NZ, near_step(g, tick), 0)
        take(g.at[pl.ds(0, NZ * BLK)], ag_core.at[tick])

    def spread(src, dst, tick, sec, first):
        def send(far, sign):
            dev = on_line((z + NZ + sign * far) % NZ, core)
            push(src, dst, ag_send.at[tick], ag_own.at[tick, z], sec, dev)

        send(REACH, 1)
        send(REACH, -1)
        for far in range(REACH - 1, 0, -1):
            send(far, 1)
            send(far, -1)
        if first == 0:
            send(0, 1)

    loads[1].wait()
    loads[2].wait()
    for tick in range(2):
        sf = st_in[tick].astype(F32)
        for kv in range(2):
            for head in range(HEADS):
                for t in range(2):
                    row = tick * 48 + (head // 2) * 8 + ((head % 2) * 2 + kv) * 2 + t
                    low = (kv * HEADS + head) * 128
                    gran_f[pl.ds(row, 1), :] = sf[t : t + 1, low : low + 128]
    st_own[...] = gran_f[...].astype(BF16)
    loads[3].wait()

    pl.semaphore_wait(barrier, 2 * REACH + 4)

    spread(g0.at[own], g0.at[own], 0, s, 1)
    relay_core(g0, 0, z)
    push(st_own, st_mate, w_send.at[1], w_recv.at[1], s, x_mate)
    push(wq.at[xl], wq.at[xl], w_send.at[0], w_recv.at[0], s, x_mate)
    loads[4].wait()
    loads[5].wait()


    times = [time_ref[s], time_ref[before]]
    lane = lax.broadcasted_iota(jnp.int32, (128, 128), 1)
    first_half = lane < 64

    def fold(tick, j):
        base = times[tick] * 3

        def step(k, sums):
            lanes = pl.ds(pl.multiple_of(k * 128, 128), 128)
            shift = mod[base, :, lanes]
            scale = mod[base + 1, :, lanes]
            w = wq[j, :, lanes].astype(F32)
            scaled = (w * (1.0 + scale)).astype(BF16)
            wide_scaled = scaled.astype(F32)
            if tick == 0:
                wmod[j, :, lanes] = scaled
            else:
                padded = jnp.concatenate([wide_scaled, jnp.zeros((8, 128), F32)], axis=0)
                low = pl.multiple_of((j * 4 + k // 6) * 80, 16)
                to = pl.ds(pl.multiple_of((k % 6) * 128, 128), 128)
                wstack[pl.ds(low, 80), to] = padded.astype(BF16)
            return sums[0] + w * shift, sums[1] + wide_scaled

        zero = jnp.zeros((QROWS, 128), F32)
        sums = lax.fori_loop(0, KC, step, (zero, zero))
        for n, value in enumerate(sums):
            total = jnp.sum(value, axis=1, keepdims=True)
            colv[tick, n, j] = jnp.broadcast_to(total, (QROWS, 128))

    fold(0, xl)

    feature = lax.broadcasted_iota(jnp.int32, (BLK, 128), 1)
    row = lax.broadcasted_iota(jnp.int32, (BLK, 128), 0)
    gate_sums = []
    for j in range(2):
        mine = (z * 4 + 2 * j + core) * BLK + row

        def gate_step(k, sums, j=j, mine=mine):
            lanes = pl.ds(pl.multiple_of(k * 128, 128), 128)
            here = feature + k * 128 == mine
            pick[pl.ds(j * BLK, BLK), lanes] = jnp.where(here, 1.0, 0.0).astype(BF16)
            return tuple(
                v + jnp.where(here, mod[times[tick] * 3 + 2, :, lanes], 0.0)
                for tick, v in enumerate(sums)
            )

        zero = jnp.zeros((BLK, 128), F32)
        sums = lax.fori_loop(0, KC, gate_step, (zero, zero))
        gate_sums.append([jnp.sum(v, axis=1, keepdims=True) for v in sums])
    for tick in range(2):
        gatev[tick] = jnp.where(first_half[:BLK], gate_sums[0][tick], gate_sums[1][tick])

    fold(1, xl)
    pf = lax.broadcasted_iota(jnp.int32, (CHUNK, 128), 0)
    po = lax.broadcasted_iota(jnp.int32, (CHUNK, 128), 1)
    for k in range(CHUNK // 128):
        to = po + (k % 3) * 128
        group = jnp.where(to >= 96, 1, 0) + jnp.where(to >= 192, 1, 0) + jnp.where(to >= 288, 1, 0)
        source = to + 96 * group + 96 * (k // 3)
        perm[:, pl.ds(k * 128, 128)] = jnp.where(pf == source, 1.0, 0.0).astype(BF16)

    @pl.when(owned == 1)
    def _():
        r = lax.broadcasted_iota(jnp.int32, (128, 128), 0)
        for j, ref in enumerate((qg_ref, kg_ref)):
            diag = jnp.where(r == lane, jnp.broadcast_to(ref[...], (128, 128)), 0.0)
            gains[j] = jnp.broadcast_to(jnp.sum(diag, axis=1, keepdims=True), (128, 128))
        pr = r[:64]
        pc = lane[:64]
        places = jnp.broadcast_to(order_ref[...].astype(F32), (64, 64))
        column = jnp.sum(
            jnp.where(pr[:, :64] == pc[:, :64], places, 0.0), axis=1, keepdims=True
        )
        token = pc % 64
        patch = ((token % LINE) // 2) * 4 + 2 * xl + token % 2
        place = jnp.sum(jnp.where(pr == patch, column, 0.0), axis=0, keepdims=True)
        pos = place * 2.0 + jnp.where(token[:1] < LINE, 0.0, 1.0)
        freq = jnp.exp(pr.astype(F32) * (-jnp.log(F32(10000.0)) / 64.0))
        angle = pos * freq
        table[0] = jnp.cos(angle)
        table[1] = jnp.sin(angle)

    def build_stale():
        take(st_mate, w_recv.at[1])
        other_f = st_mate[...].astype(F32)
        own_f = gran_f[...]
        low_f = jnp.where(xl == 0, own_f, other_f)
        high_f = jnp.where(xl == 0, other_f, own_f)
        for tick in range(2):
            for pair in range(PAIRS):
                low = tick * 48 + pair * 8
                both = jnp.concatenate([low_f[low : low + 8], high_f[low : low + 8]], axis=0)
                st_src[tick, pl.ds(pair * 16, 16), :] = both.astype(BF16)

    relay(g0, 0, 1, build_stale)
    pl.semaphore_signal(nready, inc=1, device_id=(before, p), device_id_type=MESH)

    def send_stale(tick):
        for pair in range(PAIRS):
            dev = owner_of(pair, xl)
            src = st_src.at[tick, pl.ds(pair * 16, 16)]
            dst = stale.at[tick, pl.ds(pl.multiple_of(me * 16, 16), 16)]

            @pl.when(p == dev)
            def _():
                pltpu.make_async_copy(src, dst, st_recv.at[tick]).start()

            @pl.when(p != dev)
            def _():
                push(src, dst, st_send.at[tick], st_recv.at[tick], s, dev)

    send_stale(0)


    def send_qkv(tick, j, acc, mean, var):
        static = isinstance(j, int)
        qkv = lax.rsqrt(var + 1e-06) * (acc - colv[tick, 1, j] * mean) + colv[tick, 0, j]
        qkv = qkv.astype(BF16).astype(F32)
        for i in range(9):
            top, bottom = qkv[i * 8 : i * 8 + 4], qkv[i * 8 + 4 : i * 8 + 8]
            qsrc[tick, j, i] = jnp.where(first_half[:4], top, bottom)
        for i in range(9):
            if static:
                dev, half, slot = routes[j * 9 + i]
            else:
                dev, half, slot = [
                    jnp.where(j == 0, a, b) for a, b in zip(routes[i], routes[9 + i])
                ]
            src = qsrc.at[tick, j, i]
            dst = qrecv.at[tick, half, slot]

            @pl.when(p == dev)
            def _():
                pltpu.make_async_copy(src, dst, q_recv.at[tick]).start()

            @pl.when(p != dev)
            def _():
                push(src, dst, q_send.at[tick], q_recv.at[tick], s, dev)

    for b in range(12):
        part = pl.ds(b * 128, 128)
        wide[part, :] = g0[part, :].astype(F32)
    total = jnp.zeros((64, 128), F32)
    for k in range(KC):
        lanes = pl.ds(k * 128, 128)
        piece = jnp.concatenate(
            [wide[pl.ds(t * KC + k, LINE, stride=BLK), :] for t in range(2)], axis=0
        )
        total += piece
        narrow = piece.astype(BF16)
        xr[pl.ds(0, 64), lanes] = narrow
        xr[pl.ds(64, 64), lanes] = narrow
    acc_own = dot_nt(wmod[xl], xr[...])
    mean_c = jnp.sum(total, axis=1, keepdims=True) * (1.0 / D)
    total = jnp.zeros((64, 128), F32)
    for k in range(KC):
        centred = xr[pl.ds(0, 64), pl.ds(k * 128, 128)].astype(F32) - mean_c
        total += centred * centred
    var_c = jnp.sum(total, axis=1, keepdims=True) * (1.0 / D)
    stats = jnp.where(first_half[:64], mean_c, var_c)
    stats = jnp.transpose(jnp.concatenate([stats, stats], axis=0))
    mean0, var0 = stats[0:1, :], stats[64:65, :]
    send_qkv(0, xl, acc_own, mean0, var0)
    take(wq.at[1 - xl], w_recv.at[0])
    push(wo.at[xl], wo.at[xl], w_send.at[2], w_recv.at[2], s, x_mate)
    fold(0, 1 - xl)
    send_qkv(0, 1 - xl, dot_nt(wmod[1 - xl], xr[...]), mean0, var0)
    send_stale(1)

    picked = dot_nt(pick[...], xr[...])
    residual = jnp.where(first_half[:BLK], picked[:BLK], picked[BLK:])
    fold(1, 1 - xl)
    moved = dot_nn(wstack[...], perm[...]).astype(BF16)
    half = CHUNK // 2
    for j in range(2):
        for k in range(D // CHUNK):
            rows = moved[(j * 4 + k) * 80 : (j * 4 + k + 1) * 80]
            lanes = pl.ds(k * half, half)
            wline[pl.ds(j * 160, 80), lanes] = rows[:, :half]
            wline[pl.ds(j * 160 + 80, 80), lanes] = rows[:, half:]

    def unpack_stale(tick):
        take(stale.at[tick], st_recv.at[tick])
        for b in range(4):
            part = pl.ds(b * 128, 128)
            stale_f[part, :] = stale[tick, part, :].astype(F32)
        for second in range(2):
            got = []
            for kv in range(2):
                pieces = [
                    stale_f[pl.ds(line * 8 + (second * 2 + kv) * 2 + t, LINE, stride=16), :]
                    for t in range(2)
                    for line in range(2)
                ]
                got.append(jnp.concatenate(pieces, axis=0))
            keys[tick, second] = got[0].astype(BF16)
            vals[tick, second] = jnp.transpose(got[1]).astype(BF16)

    @pl.when(owned == 1)
    def _():
        unpack_stale(0)

    def attend(tick):
        take(qrecv.at[tick], q_recv.at[tick])
        factor = 128.0 ** -0.5
        cosine, sine = table[0], table[1]

        def received(kind):
            left = first_half[:4]
            for i in range(16):
                first, second = qrecv[tick, 0, kind * 16 + i], qrecv[tick, 1, kind * 16 + i]
                merged[kind, pl.ds(i * 8, 4), :] = jnp.where(
                    left, first, pltpu.roll(second, 64, 1)
                )
                merged[kind, pl.ds(i * 8 + 4, 4), :] = jnp.where(
                    left, pltpu.roll(first, 64, 1), second
                )
            return merged[kind]

        def prepared(j):
            u = received(j)
            square = jnp.sum(u * u, axis=0, keepdims=True) * (1.0 / 128)
            u = u * lax.rsqrt(square + 1e-06) * gains[j]
            a, b = u[:64], u[64:]
            return jnp.concatenate(
                [a * cosine - b * sine, a * sine + b * cosine], axis=0
            ).astype(BF16)

        def partner(u):
            up = pltpu.roll(u, 128 - LINE, 1)
            down = pltpu.roll(u, LINE, 1)
            return jnp.where(lane % 64 < LINE, up, down)

        query = prepared(0)
        key = prepared(1).astype(F32)
        value = received(2)
        scores = jnp.where(
            first_half, dot_nn(keys[tick, 0], query), dot_nn(keys[tick, 1], query)
        ) * factor
        r = lax.broadcasted_iota(jnp.int32, (128, 128), 0)
        key_line = (r // LINE) % 2
        own_patch = (r % LINE == lane % LINE) & (key_line == xl)
        scores = jnp.where(own_patch, -1e30, scores)
        wide_q = query.astype(F32)
        same = jnp.sum(wide_q * key, axis=0, keepdims=True) * factor
        other = jnp.sum(wide_q * partner(key), axis=0, keepdims=True) * factor
        top = jnp.maximum(jnp.max(scores, axis=0, keepdims=True), jnp.maximum(same, other))
        weights = jnp.exp(scores - top)
        same = jnp.exp(same - top)
        other = jnp.exp(other - top)
        mass = jnp.sum(weights, axis=0, keepdims=True) + same + other
        weights = weights.astype(BF16)
        summed = jnp.where(
            first_half, dot_nn(vals[tick, 0], weights), dot_nn(vals[tick, 1], weights)
        )
        summed = summed + same * value + other * partner(value)
        att[tick, pair_rows(my_pair), :] = (summed / mass).astype(BF16)

    def pair_rows(pair):
        return pl.ds(pl.multiple_of(pair * 128, 128), 128)

    def send_attended(tick):
        piece = att.at[tick, pair_rows(my_pair)]

        def send(i, _):
            far = (NZ - i + 1) // 2
            dev = on_line((z + NZ + far * (2 * (i % 2) - 1)) % NZ, core)
            push(piece, piece, at_send.at[tick], at_own.at[tick, my_pair // 2], s, dev)
            return 0

        lax.fori_loop(1, NZ, send, 0)

    def gather_attended(tick):
        for j in range(3):
            pair = j * 2 + core
            piece = att.at[tick, pair_rows(pair)]

            @pl.when(owner_of(pair, xl) != p)
            def _():
                take(piece, at_own.at[tick, j])

            push(piece, piece, at_send.at[tick], at_core.at[tick], s, core_mate)
        take(att.at[tick, pl.ds(0, 3 * 128)], at_core.at[tick])

    def project(tick, residual):
        out = jnp.where(
            first_half[: 2 * BLK], dot_nn(weven[...], att[tick]), dot_nn(wodd[...], att[tick])
        )
        out = out + pltpu.roll(out, 64, 1)
        out = jnp.where(first_half[:BLK], out[:BLK], out[BLK:])
        return (residual + gatev[tick] * out).astype(BF16)

    @pl.when(owned == 1)
    def _():
        attend(0)

    @pl.when(owned == 1)
    def _():
        send_attended(0)

    take(wo.at[1 - xl], w_recv.at[2])
    for j in range(2):
        for pair in range(PAIRS):
            at = pl.ds(j * BLK, BLK), pl.ds(pair * 128, 128)
            weven[at] = wo[j, :, pl.ds(pair * 256, 128)]
            wodd[at] = wo[j, :, pl.ds(pair * 256 + 128, 128)]

    gather_attended(0)
    ysrc[...] = project(0, residual)

    pl.semaphore_wait(nready, 1)
    spread(ysrc, g1.at[own], 1, after, 0)

    relay(g1, 1, 0)
    product = dot_nn(wline[...], g1[...])
    accs = []
    for j in range(2):
        low, high = product[j * 160 : j * 160 + QROWS], product[j * 160 + 80 : j * 160 + 80 + QROWS]
        acc = jnp.where(first_half[:QROWS], low, high)
        accs.append(acc + pltpu.roll(acc, 64, 1))
    total = jnp.zeros((128, 128), F32)
    for k in range(12):
        total += g1[pl.ds(k * 128, 128), :].astype(F32)
    total = jnp.sum(total, axis=0, keepdims=True)
    mean = (total + pltpu.roll(total, 64, 1)) * (1.0 / D)
    total = jnp.zeros((128, 128), F32)
    for k in range(12):
        centred = g1[pl.ds(k * 128, 128), :].astype(F32) - mean
        total += centred * centred
    total = jnp.sum(total, axis=0, keepdims=True)
    var = (total + pltpu.roll(total, 64, 1)) * (1.0 / D)
    for j in range(2):
        send_qkv(1, j, accs[j], mean, var)

    @pl.when(owned == 1)
    def _():
        unpack_stale(1)
        attend(1)

    @pl.when(owned == 1)
    def _():
        send_attended(1)

    gather_attended(1)
    last = project(1, g1[own, :].astype(F32)).astype(F32)
    blank = jnp.zeros((16, 128), F32)
    turned = jnp.transpose(
        jnp.concatenate([last, blank, pltpu.roll(last, 64, 1), blank], axis=0)
    )
    for i in range(LINE):
        for t in range(2):
            dsrc[i, pl.ds(t, 1), :] = turned[t * LINE + i : t * LINE + i + 1, :]

    def last_send(i, _):
        to = (me + LINE // 2 + LINE + (i + 1) // 2 * (2 * (i % 2) - 1)) % LINE
        push(dsrc.at[to], drecv.at[me], d_send, d_recv, after, on_line(to // 2, to % 2))
        return 0

    lax.fori_loop(0, LINE, last_send, 0)
    take(drecv, d_recv)
    out_ref[...] = drecv[...]
    finish(8)


def per_device(states, w_qkv, w_out, mod_table, q_gain, k_gain, stale_kv, timestep, patch_order):
    hbm = pl.BlockSpec(memory_space=pl.ANY)
    vmem = pl.BlockSpec(memory_space=pltpu.VMEM)
    dma = pltpu.SemaphoreType.DMA
    regular = pltpu.SemaphoreType.REGULAR
    got = pl.pallas_call(
        kernel,
        out_shape=jax.ShapeDtypeStruct((LINE, 2, 128), F32),
        in_specs=[hbm] * 5 + [vmem] * 3 + [pl.BlockSpec(memory_space=pltpu.SMEM)],
        out_specs=vmem,
        scratch_shapes=[
            pltpu.VMEM((2, D), BF16),
            pltpu.VMEM((2, QROWS, D), BF16),
            pltpu.VMEM((2, BLK, D // 2), BF16),
            pltpu.VMEM((84, 1, D), F32),
            pltpu.VMEM((2, 2, D), BF16),
            pltpu.VMEM((BLK, 128), F32),
            pltpu.VMEM((2, 96, 128), BF16),
            pltpu.VMEM((96, 128), BF16),
            pltpu.VMEM((96, 128), BF16),
            pltpu.VMEM((96, 128), F32),
            pltpu.VMEM((LINE * BLK, 128), BF16),
            pltpu.VMEM((LINE * BLK, 128), BF16),
            pltpu.VMEM((LINE * BLK, 128), F32),
            pltpu.VMEM((128, D), BF16),
            pltpu.VMEM((2, QROWS, D), BF16),
            pltpu.VMEM((640, CHUNK), BF16),
            pltpu.VMEM((2 * BLK, D // 4), BF16),
            pltpu.VMEM((2 * BLK, D // 4), BF16),
            pltpu.VMEM((CHUNK, CHUNK), BF16),
            pltpu.VMEM((320, D // 2), BF16),
            pltpu.VMEM((2 * BLK, D), BF16),
            pltpu.VMEM((2, 2, 2, QROWS, 128), F32),
            pltpu.VMEM((2, BLK, 128), F32),
            pltpu.VMEM((2, 64, 128), F32),
            pltpu.VMEM((2, 128, 128), F32),
            pltpu.VMEM((2, 2, 9, 4, 128), F32),
            pltpu.VMEM((2, 2, 48, 4, 128), F32),
            pltpu.VMEM((3, 128, 128), F32),
            pltpu.VMEM((2, 512, 128), BF16),
            pltpu.VMEM((512, 128), F32),
            pltpu.VMEM((2, 2, 128, 128), BF16),
            pltpu.VMEM((2, 2, 128, 128), BF16),
            pltpu.VMEM((2, PAIRS * 128, 128), BF16),
            pltpu.VMEM((BLK, 128), BF16),
            pltpu.VMEM((LINE, 2, 128), F32),
            pltpu.VMEM((LINE, 2, 128), F32),
            dma((6,)),
            regular,
            dma((3,)),
            dma((3,)),
            dma((2,)),
            dma((2, NZ)),
            dma((2,)),
            dma((2,)),
            dma((2,)),
            dma((2,)),
            dma((2,)),
            dma((2,)),
            dma((2, 3)),
            dma((2,)),
            dma,
            dma,
        ],
        compiler_params=pltpu.CompilerParams(
            collective_id=0, has_side_effects=True, vmem_limit_bytes=56 * 2**20
        ),
        name="block_cycle",
    )(
        states[0],
        w_qkv[0].T,
        w_out[0].T,
        jnp.transpose(mod_table, (0, 2, 1, 3)).reshape(84, 1, D),
        stale_kv[0],
        patch_order.reshape(1, 64),
        q_gain,
        k_gain,
        timestep,
    )
    split = got.reshape(NZ, 2, 2, 2, 64)[..., :BLK]
    return jnp.transpose(split, (2, 0, 3, 1, 4)).reshape(1, 2, D).astype(BF16)


def solution(mesh):
    in_specs = (
        P("section", "patch", None),
        P("section", None, "patch"),
        P("section", None, "patch"),
        P(None, "section", None, None),
        P("section", None),
        P("section", None),
        P("section", None, "patch", None),
        P(),
        P(),
    )
    out_specs = P("section", "patch", None)
    return jax.shard_map(
        per_device, mesh=mesh, in_specs=in_specs, out_specs=out_specs, check_vma=False
    )
```

```python
import jax
import jax.numpy as jnp
from jax import lax
from jax.experimental import pallas as pl
from jax.experimental.pallas import tpu as pltpu
from jax.sharding import PartitionSpec as P

MESH = pl.DeviceIdType.MESH
F32 = jnp.float32
BF16 = jnp.bfloat16
NZ = 16
NS = 8
BLK = 48
HEADS = 12
PAIRS = 6
D = 3072
KC = D // 128
LINE = 32
QROWS = 72
REACH = 4
CHUNK = 768


def owner_of(pair, line):
    part = ((pair + line) % 3) * PAIRS + pair
    centre = (32 * part + 16) // 9
    return (centre // 4) * 4 + 2 * line + pair % 2


def dot_nt(a, b):
    return lax.dot_general(a, b, (((1,), (1,)), ((), ())), preferred_element_type=F32)


def dot_nn(a, b):
    return lax.dot_general(a, b, (((1,), (0,)), ((), ())), preferred_element_type=F32)


def kernel(
    x_hbm, wq_hbm, wo_hbm, mod_hbm, st_hbm, order_ref, qg_ref, kg_ref, time_ref,
    out_ref,
    x_in, wq, wo, mod, st_in, rows_f, st_src, st_own, st_mate, gran_f,
    g0, g1, wide, xr, wmod, wstack, wodd, weven, perm, wline, pick, colv, gatev, table, gains,
    qsrc, qrecv, merged, stale, stale_f, keys, vals, att, ysrc, dsrc, drecv,
    load_sem, nready, w_send, w_recv,
    ag_send, ag_own, ag_core,
    st_send, st_recv, q_send, q_recv,
    at_send, at_own, at_core,
    d_send, d_recv,
):
    s = lax.axis_index("section")
    p = lax.axis_index("patch")
    z = p // 4
    xl = (p // 2) % 2
    core = p % 2
    me = z * 2 + core
    after = (s + 1) % NS
    before = (s + NS - 1) % NS
    core_mate = z * 4 + xl * 2 + (1 - core)
    x_mate = z * 4 + (1 - xl) * 2 + core

    def on_line(zs, c):
        return zs * 4 + xl * 2 + c

    loads = [
        pltpu.make_async_copy(x_hbm, x_in, load_sem.at[0]),
        pltpu.make_async_copy(st_hbm.at[s], st_in.at[0], load_sem.at[1]),
        pltpu.make_async_copy(st_hbm.at[before], st_in.at[1], load_sem.at[2]),
        pltpu.make_async_copy(wq_hbm, wq.at[xl], load_sem.at[3]),
        pltpu.make_async_copy(wo_hbm, wo.at[xl], load_sem.at[4]),
        pltpu.make_async_copy(mod_hbm, mod, load_sem.at[5]),
    ]
    for load in loads:
        load.start()

    barrier = pltpu.get_barrier_semaphore()

    def greet(sec, dev):
        pl.semaphore_signal(barrier, inc=1, device_id=(sec, dev), device_id_type=MESH)

    for far in range(1, REACH + 1):
        greet(s, on_line((z + far) % NZ, core))
        greet(s, on_line((z + NZ - far) % NZ, core))
    greet(s, core_mate)
    greet(s, x_mate)
    greet(after, p)
    greet(before, p)

    loads[0].wait()
    xf = x_in[...].astype(F32)
    for t in range(2):
        for k in range(KC):
            rows_f[pl.ds(t * KC + k, 1), :] = xf[t : t + 1, k * 128 : (k + 1) * 128]
    own = pl.ds(pl.multiple_of(me * BLK, 16), BLK)
    g0[own, :] = rows_f[...].astype(BF16)
    def block(g, b):
        return g.at[pl.ds(pl.multiple_of(b * BLK, 16), BLK)]

    def push(src, dst, send, recv, sec, dev):
        pltpu.make_async_remote_copy(
            src_ref=src, dst_ref=dst, send_sem=send, recv_sem=recv,
            device_id=(sec, dev), device_id_type=MESH,
        ).start()

    def take(ref, sem):
        pltpu.make_async_copy(ref, ref, sem).wait()

    routes = []
    for j in range(2):
        for i in range(9):
            unit = (z * 4 + 2 * j + core) * 9 + i
            part = unit // 16
            head = part % HEADS
            dev = owner_of(head // 2, xl)
            routes.append((dev, head % 2, (part // HEADS) * 16 + unit % 16))

    my_pair = jnp.int32(0)
    owned = jnp.int32(0)
    for pair in range(PAIRS):
        hit = jnp.where(p == owner_of(pair, xl), 1, 0)
        my_pair = my_pair + pair * hit
        owned = owned + hit

    def drain_stale(tick):
        def step(i, _):
            take(st_src.at[tick, pl.ds(0, 16)], st_send.at[tick])
            return 0

        lax.fori_loop(0, PAIRS - owned, step, 0)

    def finish(stage):
        if stage == 1:
            for load in loads[4:]:
                load.wait()
        if stage == 2:
            @pl.when(owned == 1)
            def _():
                take(stale.at[0], st_recv.at[0])
            take(wq.at[1 - xl], w_recv.at[0])
        if 3 <= stage < 6:
            @pl.when(owned == 1)
            def _():
                take(stale.at[1], st_recv.at[1])
        if 2 <= stage < 5:
            pl.semaphore_wait(nready, 1)
        if stage >= 2:
            take(g0.at[pl.ds(0, 31 * BLK)], ag_send.at[0])
            take(wq.at[xl], w_send.at[0])
            take(wo.at[xl], w_send.at[2])

            drain_stale(0)
            take(st_own, w_send.at[1])
        if 2 <= stage < 4:
            take(wo.at[1 - xl], w_recv.at[2])
        if stage >= 3:
            drain_stale(1)
        if stage >= 5:
            take(g1, ag_send.at[1])
        if stage >= 8:
            take(dsrc, d_send)
        mine_units = jnp.int32(0)
        for dev, _, _ in routes:
            mine_units = mine_units + jnp.where(dev == p, 1, 0)
        for tick in range(2):
            def drain(i, _):
                take(qsrc.at[tick, 0, 0], q_send.at[tick])
                return 0

            if stage >= 3 + 3 * tick:
                lax.fori_loop(0, 18 - mine_units, drain, 0)
            if stage >= 4 + 3 * tick:
                def drain_piece(i, _):
                    take(att.at[tick, pl.ds(0, 128)], at_send.at[tick])
                    return 0

                lax.fori_loop(0, 3 + (NZ - 1) * owned, drain_piece, 0)

    def relay_core(g, tick, zs):
        b = zs * 2 + core
        push(block(g, b), block(g, b), ag_send.at[tick], ag_core.at[tick], s, core_mate)

    def arrive(g, tick, i):
        far = (i + 1) // 2
        zs = (z + NZ - far * (2 * (i % 2) - 1)) % NZ
        take(block(g, zs * 2 + core), ag_own.at[tick, zs])
        return zs

    def near_step(g, tick):
        def step(i, _):
            relay_core(g, tick, arrive(g, tick, i))
            return 0

        return step

    def relay(g, tick, first, between=None):
        edge = []
        for i in (2 * REACH - 1, 2 * REACH):
            zs = arrive(g, tick, i)
            edge.append(zs)
            sign = 2 * (i % 2) - 1
            piece = block(g, zs * 2 + core)
            for far in range(REACH - 1 + i % 2, 0, -1):
                dev = on_line((z + NZ + sign * far) % NZ, core)
                push(piece, piece, ag_send.at[tick], ag_own.at[tick, zs], s, dev)
        lax.fori_loop(first, 2 * REACH - 1, near_step(g, tick), 0)
        for zs in edge:
            relay_core(g, tick, zs)
        if between is not None:
            between()
        lax.fori_loop(2 * REACH + 1, NZ, near_step(g, tick), 0)
        take(g.at[pl.ds(0, NZ * BLK)], ag_core.at[tick])

    def spread(src, dst, tick, sec, first):
        def send(far, sign):
            dev = on_line((z + NZ + sign * far) % NZ, core)
            push(src, dst, ag_send.at[tick], ag_own.at[tick, z], sec, dev)

        send(REACH, 1)
        send(REACH, -1)
        for far in range(REACH - 1, 0, -1):
            send(far, 1)
            send(far, -1)
        if first == 0:
            send(0, 1)

    loads[1].wait()
    loads[2].wait()
    for tick in range(2):
        sf = st_in[tick].astype(F32)
        for kv in range(2):
            for head in range(HEADS):
                for t in range(2):
                    row = tick * 48 + (head // 2) * 8 + ((head % 2) * 2 + kv) * 2 + t
                    low = (kv * HEADS + head) * 128
                    gran_f[pl.ds(row, 1), :] = sf[t : t + 1, low : low + 128]
    st_own[...] = gran_f[...].astype(BF16)
    loads[3].wait()

    pl.semaphore_wait(barrier, 2 * REACH + 4)

    spread(g0.at[own], g0.at[own], 0, s, 1)
    relay_core(g0, 0, z)
    push(st_own, st_mate, w_send.at[1], w_recv.at[1], s, x_mate)
    push(wq.at[xl], wq.at[xl], w_send.at[0], w_recv.at[0], s, x_mate)
    loads[4].wait()
    loads[5].wait()


    times = [time_ref[s], time_ref[before]]
    lane = lax.broadcasted_iota(jnp.int32, (128, 128), 1)
    first_half = lane < 64

    def fold(tick, j):
        base = times[tick] * 3

        def step(k, sums):
            lanes = pl.ds(pl.multiple_of(k * 128, 128), 128)
            shift = mod[base, :, lanes]
            scale = mod[base + 1, :, lanes]
            w = wq[j, :, lanes].astype(F32)
            scaled = (w * (1.0 + scale)).astype(BF16)
            wide_scaled = scaled.astype(F32)
            if tick == 0:
                wmod[j, :, lanes] = scaled
            else:
                padded = jnp.concatenate([wide_scaled, jnp.zeros((8, 128), F32)], axis=0)
                low = pl.multiple_of((j * 4 + k // 6) * 80, 16)
                to = pl.ds(pl.multiple_of((k % 6) * 128, 128), 128)
                wstack[pl.ds(low, 80), to] = padded.astype(BF16)
            return sums[0] + w * shift, sums[1] + wide_scaled

        zero = jnp.zeros((QROWS, 128), F32)
        sums = lax.fori_loop(0, KC, step, (zero, zero))
        for n, value in enumerate(sums):
            total = jnp.sum(value, axis=1, keepdims=True)
            colv[tick, n, j] = jnp.broadcast_to(total, (QROWS, 128))

    fold(0, xl)

    feature = lax.broadcasted_iota(jnp.int32, (BLK, 128), 1)
    row = lax.broadcasted_iota(jnp.int32, (BLK, 128), 0)
    gate_sums = []
    for j in range(2):
        mine = (z * 4 + 2 * j + core) * BLK + row

        def gate_step(k, sums, j=j, mine=mine):
            lanes = pl.ds(pl.multiple_of(k * 128, 128), 128)
            here = feature + k * 128 == mine
            pick[pl.ds(j * BLK, BLK), lanes] = jnp.where(here, 1.0, 0.0).astype(BF16)
            return tuple(
                v + jnp.where(here, mod[times[tick] * 3 + 2, :, lanes], 0.0)
                for tick, v in enumerate(sums)
            )

        zero = jnp.zeros((BLK, 128), F32)
        sums = lax.fori_loop(0, KC, gate_step, (zero, zero))
        gate_sums.append([jnp.sum(v, axis=1, keepdims=True) for v in sums])
    for tick in range(2):
        gatev[tick] = jnp.where(first_half[:BLK], gate_sums[0][tick], gate_sums[1][tick])

    fold(1, xl)
    pf = lax.broadcasted_iota(jnp.int32, (CHUNK, 128), 0)
    po = lax.broadcasted_iota(jnp.int32, (CHUNK, 128), 1)
    for k in range(CHUNK // 128):
        to = po + (k % 3) * 128
        group = jnp.where(to >= 96, 1, 0) + jnp.where(to >= 192, 1, 0) + jnp.where(to >= 288, 1, 0)
        source = to + 96 * group + 96 * (k // 3)
        perm[:, pl.ds(k * 128, 128)] = jnp.where(pf == source, 1.0, 0.0).astype(BF16)

    @pl.when(owned == 1)
    def _():
        r = lax.broadcasted_iota(jnp.int32, (128, 128), 0)
        for j, ref in enumerate((qg_ref, kg_ref)):
            diag = jnp.where(r == lane, jnp.broadcast_to(ref[...], (128, 128)), 0.0)
            gains[j] = jnp.broadcast_to(jnp.sum(diag, axis=1, keepdims=True), (128, 128))
        pr = r[:64]
        pc = lane[:64]
        places = jnp.broadcast_to(order_ref[...].astype(F32), (64, 64))
        column = jnp.sum(
            jnp.where(pr[:, :64] == pc[:, :64], places, 0.0), axis=1, keepdims=True
        )
        token = pc % 64
        patch = ((token % LINE) // 2) * 4 + 2 * xl + token % 2
        place = jnp.sum(jnp.where(pr == patch, column, 0.0), axis=0, keepdims=True)
        pos = place * 2.0 + jnp.where(token[:1] < LINE, 0.0, 1.0)
        freq = jnp.exp(pr.astype(F32) * (-jnp.log(F32(10000.0)) / 64.0))
        angle = pos * freq
        table[0] = jnp.cos(angle)
        table[1] = jnp.sin(angle)

    def build_stale():
        take(st_mate, w_recv.at[1])
        other_f = st_mate[...].astype(F32)
        own_f = gran_f[...]
        low_f = jnp.where(xl == 0, own_f, other_f)
        high_f = jnp.where(xl == 0, other_f, own_f)
        for tick in range(2):
            for pair in range(PAIRS):
                low = tick * 48 + pair * 8
                both = jnp.concatenate([low_f[low : low + 8], high_f[low : low + 8]], axis=0)
                st_src[tick, pl.ds(pair * 16, 16), :] = both.astype(BF16)

    relay(g0, 0, 1, build_stale)
    pl.semaphore_signal(nready, inc=1, device_id=(before, p), device_id_type=MESH)

    def send_stale(tick):
        for pair in range(PAIRS):
            dev = owner_of(pair, xl)
            src = st_src.at[tick, pl.ds(pair * 16, 16)]
            dst = stale.at[tick, pl.ds(pl.multiple_of(me * 16, 16), 16)]

            @pl.when(p == dev)
            def _():
                pltpu.make_async_copy(src, dst, st_recv.at[tick]).start()

            @pl.when(p != dev)
            def _():
                push(src, dst, st_send.at[tick], st_recv.at[tick], s, dev)

    send_stale(0)


    def send_qkv(tick, j, acc, mean, var):
        static = isinstance(j, int)
        qkv = lax.rsqrt(var + 1e-06) * (acc - colv[tick, 1, j] * mean) + colv[tick, 0, j]
        qkv = qkv.astype(BF16).astype(F32)
        for i in range(9):
            top, bottom = qkv[i * 8 : i * 8 + 4], qkv[i * 8 + 4 : i * 8 + 8]
            qsrc[tick, j, i] = jnp.where(first_half[:4], top, bottom)
        for i in range(9):
            if static:
                dev, half, slot = routes[j * 9 + i]
            else:
                dev, half, slot = [
                    jnp.where(j == 0, a, b) for a, b in zip(routes[i], routes[9 + i])
                ]
            src = qsrc.at[tick, j, i]
            dst = qrecv.at[tick, half, slot]

            @pl.when(p == dev)
            def _():
                pltpu.make_async_copy(src, dst, q_recv.at[tick]).start()

            @pl.when(p != dev)
            def _():
                push(src, dst, q_send.at[tick], q_recv.at[tick], s, dev)

    for b in range(12):
        part = pl.ds(b * 128, 128)
        wide[part, :] = g0[part, :].astype(F32)
    total = jnp.zeros((64, 128), F32)
    for k in range(KC):
        lanes = pl.ds(k * 128, 128)
        piece = jnp.concatenate(
            [wide[pl.ds(t * KC + k, LINE, stride=BLK), :] for t in range(2)], axis=0
        )
        total += piece
        narrow = piece.astype(BF16)
        xr[pl.ds(0, 64), lanes] = narrow
        xr[pl.ds(64, 64), lanes] = narrow
    acc_own = dot_nt(wmod[xl], xr[...])
    mean_c = jnp.sum(total, axis=1, keepdims=True) * (1.0 / D)
    total = jnp.zeros((64, 128), F32)
    for k in range(KC):
        centred = xr[pl.ds(0, 64), pl.ds(k * 128, 128)].astype(F32) - mean_c
        total += centred * centred
    var_c = jnp.sum(total, axis=1, keepdims=True) * (1.0 / D)
    stats = jnp.where(first_half[:64], mean_c, var_c)
    stats = jnp.transpose(jnp.concatenate([stats, stats], axis=0))
    mean0, var0 = stats[0:1, :], stats[64:65, :]
    send_qkv(0, xl, acc_own, mean0, var0)
    take(wq.at[1 - xl], w_recv.at[0])
    push(wo.at[xl], wo.at[xl], w_send.at[2], w_recv.at[2], s, x_mate)
    fold(0, 1 - xl)
    send_qkv(0, 1 - xl, dot_nt(wmod[1 - xl], xr[...]), mean0, var0)

    picked = dot_nt(pick[...], xr[...])
    residual = jnp.where(first_half[:BLK], picked[:BLK], picked[BLK:])
    fold(1, 1 - xl)
    moved = dot_nn(wstack[...], perm[...]).astype(BF16)
    half = CHUNK // 2
    for j in range(2):
        for k in range(D // CHUNK):
            rows = moved[(j * 4 + k) * 80 : (j * 4 + k + 1) * 80]
            lanes = pl.ds(k * half, half)
            wline[pl.ds(j * 160, 80), lanes] = rows[:, :half]
            wline[pl.ds(j * 160 + 80, 80), lanes] = rows[:, half:]
    send_stale(1)

    def unpack_stale(tick):
        take(stale.at[tick], st_recv.at[tick])
        for b in range(4):
            part = pl.ds(b * 128, 128)
            stale_f[part, :] = stale[tick, part, :].astype(F32)
        for second in range(2):
            got = []
            for kv in range(2):
                pieces = [
                    stale_f[pl.ds(line * 8 + (second * 2 + kv) * 2 + t, LINE, stride=16), :]
                    for t in range(2)
                    for line in range(2)
                ]
                got.append(jnp.concatenate(pieces, axis=0))
            keys[tick, second] = got[0].astype(BF16)
            vals[tick, second] = jnp.transpose(got[1]).astype(BF16)

    @pl.when(owned == 1)
    def _():
        unpack_stale(0)

    def attend(tick):
        take(qrecv.at[tick], q_recv.at[tick])
        factor = 128.0 ** -0.5
        cosine, sine = table[0], table[1]

        def received(kind):
            left = first_half[:4]
            for i in range(16):
                first, second = qrecv[tick, 0, kind * 16 + i], qrecv[tick, 1, kind * 16 + i]
                merged[kind, pl.ds(i * 8, 4), :] = jnp.where(
                    left, first, pltpu.roll(second, 64, 1)
                )
                merged[kind, pl.ds(i * 8 + 4, 4), :] = jnp.where(
                    left, pltpu.roll(first, 64, 1), second
                )
            return merged[kind]

        def prepared(j):
            u = received(j)
            square = jnp.sum(u * u, axis=0, keepdims=True) * (1.0 / 128)
            u = u * lax.rsqrt(square + 1e-06) * gains[j]
            a, b = u[:64], u[64:]
            return jnp.concatenate(
                [a * cosine - b * sine, a * sine + b * cosine], axis=0
            ).astype(BF16)

        def partner(u):
            up = pltpu.roll(u, 128 - LINE, 1)
            down = pltpu.roll(u, LINE, 1)
            return jnp.where(lane % 64 < LINE, up, down)

        query = prepared(0)
        key = prepared(1).astype(F32)
        value = received(2)
        scores = jnp.where(
            first_half, dot_nn(keys[tick, 0], query), dot_nn(keys[tick, 1], query)
        ) * factor
        r = lax.broadcasted_iota(jnp.int32, (128, 128), 0)
        key_line = (r // LINE) % 2
        own_patch = (r % LINE == lane % LINE) & (key_line == xl)
        scores = jnp.where(own_patch, -1e30, scores)
        wide_q = query.astype(F32)
        same = jnp.sum(wide_q * key, axis=0, keepdims=True) * factor
        other = jnp.sum(wide_q * partner(key), axis=0, keepdims=True) * factor
        top = jnp.maximum(jnp.max(scores, axis=0, keepdims=True), jnp.maximum(same, other))
        weights = jnp.exp(scores - top)
        same = jnp.exp(same - top)
        other = jnp.exp(other - top)
        mass = jnp.sum(weights, axis=0, keepdims=True) + same + other
        weights = weights.astype(BF16)
        summed = jnp.where(
            first_half, dot_nn(vals[tick, 0], weights), dot_nn(vals[tick, 1], weights)
        )
        summed = summed + same * value + other * partner(value)
        att[tick, pair_rows(my_pair), :] = (summed / mass).astype(BF16)

    def pair_rows(pair):
        return pl.ds(pl.multiple_of(pair * 128, 128), 128)

    def send_attended(tick):
        piece = att.at[tick, pair_rows(my_pair)]

        def send(i, _):
            far = (NZ - i + 1) // 2
            dev = on_line((z + NZ + far * (2 * (i % 2) - 1)) % NZ, core)
            push(piece, piece, at_send.at[tick], at_own.at[tick, my_pair // 2], s, dev)
            return 0

        lax.fori_loop(1, NZ, send, 0)

    def gather_attended(tick):
        for j in range(3):
            pair = j * 2 + core
            piece = att.at[tick, pair_rows(pair)]

            @pl.when(owner_of(pair, xl) != p)
            def _():
                take(piece, at_own.at[tick, j])

            push(piece, piece, at_send.at[tick], at_core.at[tick], s, core_mate)
        take(att.at[tick, pl.ds(0, 3 * 128)], at_core.at[tick])

    def project(tick, residual):
        out = jnp.where(
            first_half[: 2 * BLK], dot_nn(weven[...], att[tick]), dot_nn(wodd[...], att[tick])
        )
        out = out + pltpu.roll(out, 64, 1)
        out = jnp.where(first_half[:BLK], out[:BLK], out[BLK:])
        return (residual + gatev[tick] * out).astype(BF16)

    @pl.when(owned == 1)
    def _():
        attend(0)

    @pl.when(owned == 1)
    def _():
        send_attended(0)

    take(wo.at[1 - xl], w_recv.at[2])
    for j in range(2):
        for pair in range(PAIRS):
            at = pl.ds(j * BLK, BLK), pl.ds(pair * 128, 128)
            weven[at] = wo[j, :, pl.ds(pair * 256, 128)]
            wodd[at] = wo[j, :, pl.ds(pair * 256 + 128, 128)]

    gather_attended(0)
    ysrc[...] = project(0, residual)

    pl.semaphore_wait(nready, 1)
    spread(ysrc, g1.at[own], 1, after, 0)

    relay(g1, 1, 0)
    product = dot_nn(wline[...], g1[...])
    accs = []
    for j in range(2):
        low, high = product[j * 160 : j * 160 + QROWS], product[j * 160 + 80 : j * 160 + 80 + QROWS]
        acc = jnp.where(first_half[:QROWS], low, high)
        accs.append(acc + pltpu.roll(acc, 64, 1))
    total = jnp.zeros((128, 128), F32)
    for k in range(12):
        total += g1[pl.ds(k * 128, 128), :].astype(F32)
    total = jnp.sum(total, axis=0, keepdims=True)
    mean = (total + pltpu.roll(total, 64, 1)) * (1.0 / D)
    total = jnp.zeros((128, 128), F32)
    for k in range(12):
        centred = g1[pl.ds(k * 128, 128), :].astype(F32) - mean
        total += centred * centred
    total = jnp.sum(total, axis=0, keepdims=True)
    var = (total + pltpu.roll(total, 64, 1)) * (1.0 / D)
    for j in range(2):
        send_qkv(1, j, accs[j], mean, var)

    @pl.when(owned == 1)
    def _():
        unpack_stale(1)
        attend(1)

    @pl.when(owned == 1)
    def _():
        send_attended(1)

    gather_attended(1)
    last = project(1, g1[own, :].astype(F32)).astype(F32)
    blank = jnp.zeros((16, 128), F32)
    turned = jnp.transpose(
        jnp.concatenate([last, blank, pltpu.roll(last, 64, 1), blank], axis=0)
    )
    for i in range(LINE):
        for t in range(2):
            dsrc[i, pl.ds(t, 1), :] = turned[t * LINE + i : t * LINE + i + 1, :]

    def last_send(i, _):
        to = (me + LINE // 2 + LINE + (i + 1) // 2 * (2 * (i % 2) - 1)) % LINE
        push(dsrc.at[to], drecv.at[me], d_send, d_recv, after, on_line(to // 2, to % 2))
        return 0

    lax.fori_loop(0, LINE, last_send, 0)
    take(drecv, d_recv)
    out_ref[...] = drecv[...]
    finish(8)


def per_device(states, w_qkv, w_out, mod_table, q_gain, k_gain, stale_kv, timestep, patch_order):
    hbm = pl.BlockSpec(memory_space=pl.ANY)
    vmem = pl.BlockSpec(memory_space=pltpu.VMEM)
    dma = pltpu.SemaphoreType.DMA
    regular = pltpu.SemaphoreType.REGULAR
    got = pl.pallas_call(
        kernel,
        out_shape=jax.ShapeDtypeStruct((LINE, 2, 128), F32),
        in_specs=[hbm] * 5 + [vmem] * 3 + [pl.BlockSpec(memory_space=pltpu.SMEM)],
        out_specs=vmem,
        scratch_shapes=[
            pltpu.VMEM((2, D), BF16),
            pltpu.VMEM((2, QROWS, D), BF16),
            pltpu.VMEM((2, BLK, D // 2), BF16),
            pltpu.VMEM((84, 1, D), F32),
            pltpu.VMEM((2, 2, D), BF16),
            pltpu.VMEM((BLK, 128), F32),
            pltpu.VMEM((2, 96, 128), BF16),
            pltpu.VMEM((96, 128), BF16),
            pltpu.VMEM((96, 128), BF16),
            pltpu.VMEM((96, 128), F32),
            pltpu.VMEM((LINE * BLK, 128), BF16),
            pltpu.VMEM((LINE * BLK, 128), BF16),
            pltpu.VMEM((LINE * BLK, 128), F32),
            pltpu.VMEM((128, D), BF16),
            pltpu.VMEM((2, QROWS, D), BF16),
            pltpu.VMEM((640, CHUNK), BF16),
            pltpu.VMEM((2 * BLK, D // 4), BF16),
            pltpu.VMEM((2 * BLK, D // 4), BF16),
            pltpu.VMEM((CHUNK, CHUNK), BF16),
            pltpu.VMEM((320, D // 2), BF16),
            pltpu.VMEM((2 * BLK, D), BF16),
            pltpu.VMEM((2, 2, 2, QROWS, 128), F32),
            pltpu.VMEM((2, BLK, 128), F32),
            pltpu.VMEM((2, 64, 128), F32),
            pltpu.VMEM((2, 128, 128), F32),
            pltpu.VMEM((2, 2, 9, 4, 128), F32),
            pltpu.VMEM((2, 2, 48, 4, 128), F32),
            pltpu.VMEM((3, 128, 128), F32),
            pltpu.VMEM((2, 512, 128), BF16),
            pltpu.VMEM((512, 128), F32),
            pltpu.VMEM((2, 2, 128, 128), BF16),
            pltpu.VMEM((2, 2, 128, 128), BF16),
            pltpu.VMEM((2, PAIRS * 128, 128), BF16),
            pltpu.VMEM((BLK, 128), BF16),
            pltpu.VMEM((LINE, 2, 128), F32),
            pltpu.VMEM((LINE, 2, 128), F32),
            dma((6,)),
            regular,
            dma((3,)),
            dma((3,)),
            dma((2,)),
            dma((2, NZ)),
            dma((2,)),
            dma((2,)),
            dma((2,)),
            dma((2,)),
            dma((2,)),
            dma((2,)),
            dma((2, 3)),
            dma((2,)),
            dma,
            dma,
        ],
        compiler_params=pltpu.CompilerParams(
            collective_id=0, has_side_effects=True, vmem_limit_bytes=56 * 2**20
        ),
        name="block_cycle",
    )(
        states[0],
        w_qkv[0].T,
        w_out[0].T,
        jnp.transpose(mod_table, (0, 2, 1, 3)).reshape(84, 1, D),
        stale_kv[0],
        patch_order.reshape(1, 64),
        q_gain,
        k_gain,
        timestep,
    )
    split = got.reshape(NZ, 2, 2, 2, 64)[..., :BLK]
    return jnp.transpose(split, (2, 0, 3, 1, 4)).reshape(1, 2, D).astype(BF16)


def solution(mesh):
    in_specs = (
        P("section", "patch", None),
        P("section", None, "patch"),
        P("section", None, "patch"),
        P(None, "section", None, None),
        P("section", None),
        P("section", None),
        P("section", None, "patch", None),
        P(),
        P(),
    )
    out_specs = P("section", "patch", None)
    return jax.shard_map(
        per_device, mesh=mesh, in_specs=in_specs, out_specs=out_specs, check_vma=False
    )
```
